256 devices in a mesh: grp: 8 (over y, core), wide: 32 (over z, x).
Axes of the slice: x: 4, y: 4, z: 8, core: 2. Of those that a mesh axis runs over, the one named last changes fastest.
Arguments:
- features: bfloat16 [2048, 128, 128], P(('grp', 'wide')), may hold values from -6 to 6
- group_src: int32 [2048, 8], P(('grp', 'wide')), may hold values from 0 to 63
- group_count: int32 [2048], P(('grp', 'wide')), may hold values from 1 to 8
- group_tiles: bfloat16 [2048, 8, 128, 128], P(('grp', 'wide')), may hold values from 0 to 2, as said below
- hist_owner: int32 [2048, 4, 1], P(('grp', 'wide')), may hold values from 0 to 31; in each aligned block of 32 rows (0 to 31, 32 to 63, ..., all dimensions but the last counted through in order) at most 2 rows name the same one
- hist_local: int32 [2048, 4], P(('grp', 'wide')), may hold values from 0 to 3
- hist_count: int32 [2048], P(('grp', 'wide')), may hold values from 1 to 4
- hist_tiles: bfloat16 [2048, 4, 128, 128], P(('grp', 'wide')), may hold values from 0 to 2, as said below
- feature_store: bfloat16 [128, 128, 128], P('wide'), may hold values from -6 to 6
- hidden_store: bfloat16 [128, 128, 256], P('wide'), may hold values from -4 to 4
- self_one: bfloat16 [128, 256], replicated, may hold values from -0.5 to 0.5
- neigh_one: bfloat16 [128, 256], replicated, may hold values from -2 to 2
- self_two: bfloat16 [256, 256], replicated, may hold values from -0.375 to 0.375
- neigh_two: bfloat16 [256, 256], replicated, may hold values from -1.5 to 1.5
- cotangent: bfloat16 [2048, 128, 256], P(('grp', 'wide')), may hold values from -0.01171875 to 0.01171875
Outputs:
- embedding: bfloat16 [2048, 128, 256], P(('grp', 'wide'))
- grad_self_one: float32 [128, 256], replicated
- grad_neigh_one: float32 [128, 256], replicated
- grad_self_two: float32 [256, 256], replicated
- grad_neigh_two: float32 [256, 256], replicated
The draws below stay inside these ranges and needn't reach their ends.
Inputs may be any that keep to these rules, and one draw needn't show every extreme that they name: `group_src`: index of a cluster within the group of the slot's batch cluster. `hist_owner`: among the 8 x 4 history slots of one device, no owner is named more than 2 times. `group_tiles`: nonnegative edge weights. `hist_tiles`: nonnegative edge weights.
All inputs are finite; a program needn't handle non-finite values.
Results may differ from the reference program's by a relative error of at most 0.009.
Values may be sent and summed in bfloat16 or wider, within the bound.
A program may use at most 128 MiB of HBM per device.

```python
import math
import jax
import jax.numpy as jnp
import numpy as np
from jax import lax

F0 = 128
HID = 256
BLOCK = 128
C_DEV = 8
S_IN = 8
S_H = 4
HB_DEV = 4
CLUSTERS = 2048
GC = 64
HIST = 128
NODES = 262144
CAP = 2
N_GRP = 8
N_WIDE = 32


def sparse_tiles(key, shape):
    keep = jax.random.bernoulli(jax.random.fold_in(key, 1), 1.0 / 16.0, shape).astype(jnp.float32)
    values = jax.random.uniform(jax.random.fold_in(key, 2), shape, jnp.float32, 0.5, 1.5)
    return (keep * values).astype(jnp.bfloat16)


def draw_group_tiles(key, part):
    key = jax.random.fold_in(key, 11)
    return sparse_tiles(key, (CLUSTERS, S_IN, BLOCK, BLOCK))


def draw_hist_tiles(key, part):
    key = jax.random.fold_in(key, 23)
    return sparse_tiles(key, (CLUSTERS, S_H, BLOCK, BLOCK))


def place_ends(values, own_key, least, high):
    longest = values.shape.index(max(values.shape))
    spots = []
    for shift in (0, 1):
        where = [jax.random.randint(jax.random.fold_in(own_key, axis), (), 0, length) for axis, length in enumerate(values.shape)]
        where[longest] = (where[longest] + shift) % values.shape[longest]
        spots.append(tuple(where))
    return values.at[spots[0]].set(least).at[spots[1]].set(high)


def shard_levels(own_key, extent, pieces, smallest, largest):
    def one(position, parts):
        draws = jax.random.uniform(jax.random.fold_in(jax.random.fold_in(own_key, 6), position), (parts,), jnp.float32, smallest / len(pieces), largest / len(pieces))
        return jnp.repeat(jnp.exp(draws), extent[position] // parts).reshape((-1,) + (1,) * (len(extent) - position - 1))

    factor_of = one(*pieces[0])
    for cut in pieces[1:]:
        factor_of = factor_of * one(*cut)
    return factor_of


def deal_out(stream_key, own, number, rows, number_of, top, bound, lean):
    sequence = jax.random.permutation(stream_key, number_of)
    crowded, ordinary = load_shares(number_of, rows * top, bound, lean, True), load_shares(number_of, rows * top, bound, lean, False)
    places = jnp.arange(number_of)

    def named(sizes, offset_by):
        used = int((sizes > 0).sum())
        fixed = max(1, used // 4)
        moved = fixed + (places - fixed + offset_by * (used - fixed)) % max(1, number_of - fixed)
        return jnp.zeros((number_of,), jnp.int32).at[sequence[jnp.where(places < fixed, places, moved)]].set(jnp.asarray(sizes, jnp.int32))

    sizes = jnp.where(number % 4 == 0, named(crowded, number // 4), named(ordinary, number - number // 4 - 1))
    mixed = jax.random.permutation(jax.random.fold_in(own, 3), number_of)
    giver, sink = mixed[0:number_of // 2 * 2:2], mixed[1:number_of // 2 * 2:2]
    slack = jnp.minimum(sizes[giver] - 1, bound - sizes[sink]) // 2
    slack = jnp.where((giver == sequence[0]) | (sink == sequence[0]) | (sizes[sink] == 0), 0, jnp.maximum(slack, 0))
    moved = jax.random.randint(jax.random.fold_in(own, 4), (number_of // 2,), 0, 1 << 20) % (slack + 1)
    sizes = sizes.at[giver].add(-moved).at[sink].add(moved)
    labels = jnp.searchsorted(jnp.cumsum(sizes), jnp.arange(rows * top), side="right").astype(jnp.int32)
    grid = labels.reshape(top, rows).T
    grid = grid[jax.random.permutation(jax.random.fold_in(own, 1), rows)]
    offset_by = jax.random.randint(jax.random.fold_in(own, 2), (rows, 1), 0, top)
    return jnp.take_along_axis(grid, (jnp.arange(top)[None, :] + offset_by) % top, axis=1)


def load_shares(number_of, total, bound, skew, full):
    portions = [(1 << 20) // math.isqrt(grade ** skew) + 1 for grade in range(1, number_of + 1)]
    largest = bound if full else min(bound, max(-(-total // number_of), total * portions[0] // sum(portions)))
    least = 1 if total - largest >= number_of - 1 else 0
    given, surplus = [largest] + [least] * (number_of - 1), total - largest - least * (number_of - 1)
    while surplus > 0:
        candidates = [i for i in range(1, number_of) if given[i] < largest] or [i for i in range(1, number_of) if given[i] < bound]
        pool, remaining = sum([portions[i] for i in candidates]), surplus
        for i in candidates:
            addition = min(bound - given[i], max(1, remaining * portions[i] // pool), surplus)
            given[i] = given[i] + addition
            surplus = surplus - addition
    return np.array(given)


def noise(stream_key, dims, width, most, cuts=(), kind=jnp.bfloat16):
    result = jax.random.normal(stream_key, dims, jnp.float32) * width
    if len(cuts) > 0:
        result = shard_levels(stream_key, dims, cuts, -0.22, 0.18) * result
    return jnp.clip(result, min=-most, max=most).astype(kind)


def setup_inputs(seed: int = 0) -> dict:
    seeds = jax.random.split(jax.random.key(seed), 16)
    features = noise(seeds[0], (CLUSTERS, BLOCK, F0), 1.0, 6.0, ((0, 256),))
    group_src = place_ends(jax.random.randint(seeds[1], (CLUSTERS, S_IN), 0, GC), jax.random.fold_in(seeds[1], 1), 0, GC - 1).astype(jnp.int32)
    group_count = place_ends(jax.random.randint(seeds[2], (CLUSTERS,), 1, S_IN + 1), jax.random.fold_in(seeds[2], 1), 1, S_IN).astype(jnp.int32)
    group_tiles = draw_group_tiles(jax.random.fold_in(seeds[15], 71), 0)
    hist_owner_keys = jax.random.split(jax.random.fold_in(seeds[4], 1), CLUSTERS * S_H // (C_DEV * S_H))
    hist_owner_turns = jax.random.permutation(jax.random.fold_in(seeds[4], 3), CLUSTERS * S_H // (C_DEV * S_H))
    hist_owner = jax.vmap(lambda own, number: deal_out(jax.random.fold_in(seeds[4], 2), own, number, C_DEV * S_H, N_WIDE, 1, CAP, 2))(hist_owner_keys, hist_owner_turns).reshape((CLUSTERS, S_H, 1))
    hist_local = place_ends(jax.random.randint(seeds[5], (CLUSTERS, S_H), 0, HB_DEV), jax.random.fold_in(seeds[5], 1), 0, HB_DEV - 1).astype(jnp.int32)
    hist_count = place_ends(jax.random.randint(seeds[6], (CLUSTERS,), 1, S_H + 1), jax.random.fold_in(seeds[6], 1), 1, S_H).astype(jnp.int32)
    hist_tiles = draw_hist_tiles(jax.random.fold_in(seeds[15], 71), 0)
    feature_store = noise(seeds[8], (HIST, BLOCK, F0), 1.0, 6.0, ((0, 32),))
    hidden_store = noise(seeds[9], (HIST, BLOCK, HID), 0.5, 4.0, ((0, 32),))
    self_one = noise(seeds[10], (F0, HID), F0 ** -0.5, 0.5)
    neigh_one = noise(seeds[11], (F0, HID), (F0 // 16) ** -0.5, 2.0)
    self_two = noise(seeds[12], (HID, HID), HID ** -0.5, 0.375)
    neigh_two = noise(seeds[13], (HID, HID), (HID // 16) ** -0.5, 1.5)
    cotangent = noise(seeds[14], (CLUSTERS, BLOCK, HID), NODES ** -0.5, 0.01171875, ((0, 256),))
    return dict(features=features, group_src=group_src, group_count=group_count, group_tiles=group_tiles, hist_owner=hist_owner, hist_local=hist_local, hist_count=hist_count, hist_tiles=hist_tiles, feature_store=feature_store, hidden_store=hidden_store, self_one=self_one, neigh_one=neigh_one, self_two=self_two, neigh_two=neigh_two, cotangent=cotangent)


def neighbor_mean(near, far, live_a, live_b, group_tiles, hist_tiles, near_table, far_table):
    def single(index):
        tiles_a = group_tiles[index].astype(jnp.float32) * live_a[index][:, None, None]
        tiles_b = hist_tiles[index].astype(jnp.float32) * live_b[index][:, None, None]
        blocks_a = near_table[near[index]].astype(jnp.float32)
        blocks_b = far_table[far[index]].astype(jnp.float32)
        total = jnp.einsum('srj,sjf->rf', tiles_a, blocks_a, precision=lax.Precision.HIGHEST)
        total = total + jnp.einsum('srj,sjf->rf', tiles_b, blocks_b, precision=lax.Precision.HIGHEST)
        degree = 1.0 + jnp.sum(tiles_a, axis=(0, 2)) + jnp.sum(tiles_b, axis=(0, 2))
        return (total / degree[:, None]).astype(jnp.bfloat16), degree
    return lax.map(single, jnp.arange(CLUSTERS).astype(jnp.int32))


def reference(features, group_src, group_count, group_tiles, hist_owner, hist_local, hist_count, hist_tiles, feature_store, hidden_store, self_one, neigh_one, self_two, neigh_two, cotangent):
    device = jnp.arange(CLUSTERS).astype(jnp.int32) // C_DEV
    column = device % N_WIDE
    near = ((group_src // C_DEV) * N_WIDE + column[:, None]) * C_DEV + group_src % C_DEV
    far = hist_owner[:, :, 0] * HB_DEV + hist_local
    live_a = (jnp.arange(S_IN)[None, :] < group_count[:, None]).astype(jnp.float32)
    live_b = (jnp.arange(S_H)[None, :] < hist_count[:, None]).astype(jnp.float32)
    mean_one, degree = neighbor_mean(near, far, live_a, live_b, group_tiles, hist_tiles, features, feature_store)
    flat = features.reshape(NODES, F0)
    mean_flat = mean_one.reshape(NODES, F0)
    pre_one = jnp.dot(flat, self_one, preferred_element_type=jnp.float32) + jnp.dot(mean_flat, neigh_one, preferred_element_type=jnp.float32)
    hidden = jax.nn.silu(pre_one).astype(jnp.bfloat16)
    hidden_blocks = hidden.reshape(CLUSTERS, BLOCK, HID)
    mean_two, unused = neighbor_mean(near, far, live_a, live_b, group_tiles, hist_tiles, hidden_blocks, hidden_store)
    mean_two_flat = mean_two.reshape(NODES, HID)
    pre_two = jnp.dot(hidden, self_two, preferred_element_type=jnp.float32) + jnp.dot(mean_two_flat, neigh_two, preferred_element_type=jnp.float32)
    embedding = pre_two.astype(jnp.bfloat16).reshape(CLUSTERS, BLOCK, HID)
    upstream = cotangent.reshape(NODES, HID)
    grad_self_two = jnp.dot(hidden.T, upstream, preferred_element_type=jnp.float32)
    grad_neigh_two = jnp.dot(mean_two_flat.T, upstream, preferred_element_type=jnp.float32)
    through_neigh = jnp.dot(upstream, neigh_two.T, preferred_element_type=jnp.float32)
    scaled = (through_neigh.reshape(CLUSTERS, BLOCK, HID) / degree[:, :, None]).astype(jnp.bfloat16)

    def per_group(column_index):
        def per_device(row_index):
            dev = row_index * N_WIDE + column_index
            start = dev * C_DEV
            tiles_a = lax.dynamic_slice_in_dim(group_tiles, start, C_DEV, 0).astype(jnp.float32)
            mask_a = lax.dynamic_slice_in_dim(live_a, start, C_DEV, 0)
            tiles_a = tiles_a * mask_a[:, :, None, None]
            grads = lax.dynamic_slice_in_dim(scaled, start, C_DEV, 0).astype(jnp.float32)
            terms = jnp.einsum('csrj,crf->csjf', tiles_a, grads, precision=lax.Precision.HIGHEST)
            targets = lax.dynamic_slice_in_dim(group_src, start, C_DEV, 0).reshape(-1)
            pick = (jnp.arange(GC)[:, None] == targets[None, :]).astype(jnp.float32)
            partial_value = jnp.einsum('gx,xjf->gjf', pick, terms.reshape(C_DEV * S_IN, BLOCK, HID), precision=lax.Precision.HIGHEST)
            return partial_value.astype(jnp.bfloat16)
        partials = lax.map(per_device, jnp.arange(N_GRP).astype(jnp.int32))
        return jnp.sum(partials.astype(jnp.float32), axis=0)

    returned = lax.map(per_group, jnp.arange(N_WIDE).astype(jnp.int32))
    returned = returned.reshape(N_WIDE, N_GRP, C_DEV, BLOCK, HID).transpose(1, 0, 2, 3, 4).reshape(NODES, HID)
    total = jnp.dot(upstream, self_two.T, preferred_element_type=jnp.float32) + returned
    sigma = jax.nn.sigmoid(pre_one)
    grad_pre = (total * sigma * (1.0 + pre_one * (1.0 - sigma))).astype(jnp.bfloat16)
    grad_self_one = jnp.dot(flat.T, grad_pre, preferred_element_type=jnp.float32)
    grad_neigh_one = jnp.dot(mean_flat.T, grad_pre, preferred_element_type=jnp.float32)
    return (embedding, grad_self_one, grad_neigh_one, grad_self_two, grad_neigh_two)
```

```python
import jax
import jax.numpy as jnp
from jax import lax
from jax.experimental import pallas as pl
from jax.experimental.pallas import tpu as pltpu
from jax.sharding import PartitionSpec as P

MESH = pl.DeviceIdType.MESH
F32 = jnp.float32
BF16 = jnp.bfloat16
NX, NY, NZ = 4, 4, 8


def prep_kernel(gsrc, gcnt, howner, hlocal, hcnt, out, seen, start):
    @pl.loop(0, 64)
    def _(i):
        seen[i] = 0

    @pl.loop(0, 8)
    def _(k):
        for s in range(8):
            t = gsrc[k, s]
            out[5, k * 8 + s] = t
            seen[t] = seen[t] + 1
        for s in range(4):
            out[6, k * 4 + s] = howner[k, s, 0] * 4 + hlocal[k, s]
        out[7, k] = gcnt[k]
        out[7, 8 + k] = hcnt[k]

    def scan(g, base):
        start[g] = base
        many = seen[g]
        out[3, g] = jnp.maximum(base + many - 1, 0)
        out[4, g] = jnp.minimum(many, 1)
        seen[g] = 0
        return base + many

    lax.fori_loop(0, 64, scan, jnp.int32(0))

    @pl.loop(0, 8)
    def _(k):
        for s in range(8):
            t = gsrc[k, s]
            place = start[t] + seen[t]
            out[0, place] = k * 8 + s
            out[1, place] = k
            out[2, place] = jnp.minimum(seen[t], 1)
            seen[t] = seen[t] + 1


def prep(gsrc, gcnt, howner, hlocal, hcnt):
    smem = pl.BlockSpec(memory_space=pltpu.SMEM)
    return pl.pallas_call(
        prep_kernel,
        out_shape=jax.ShapeDtypeStruct((8, 64), jnp.int32),
        in_specs=[smem] * 5,
        out_specs=smem,
        scratch_shapes=[pltpu.SMEM((64,), jnp.int32), pltpu.SMEM((64,), jnp.int32)],
    )(gsrc, gcnt, howner, hlocal, hcnt)


def dot(a, b):
    return jnp.dot(a, b, preferred_element_type=F32)


def dot_t(a, b):
    return lax.dot_general(a, b, (((0,), (0,)), ((), ())), preferred_element_type=F32)


def dot_nt(a, b):
    return lax.dot_general(a, b, (((1,), (1,)), ((), ())), preferred_element_type=F32)


def main_kernel(
    sc, features, gtiles, htiles, fstore, hstore, s1_h, n1_h, s2_h, n2_h, cot_h,
    emb, gs1, gn1, gs2, gn2,
    GF, GM, GH, HF, HH, TA, TB, COT, S1, N1, S2, N2,
    INV, SC, RT, PS, PR, Q, T1, FR, RB, ACC, PRE, HO, FAR, MF,
    G, GP, B1, Q1, B2, Q2, B3, B4, FG,
    load_sem, ysem_s, ysem_r, sib_s, sib_r, axs, axr, azs, azr, bzs, bzr, bxs, bxr,
    rs_s, rs_r, ps_s, ps_r, a_s, a_r, b2s, b2r, b3s, b3r, b4s, b4r, b5s, b5r, b6s, b6r,
):
    grp = lax.axis_index("grp")
    wide = lax.axis_index("wide")
    z, x = wide // NX, wide % NX
    y, c = grp // 2, grp % 2
    o = 1 - c

    def at(dz=0, dy=0, dx=0):
        return (((y + dy) % NY) * 2 + c, ((z + dz) % NZ) * NX + (x + dx) % NX)

    sib = (y * 2 + o, wide)
    pending = []

    def send(src, dst, ss, rs, dev):
        cp = pltpu.make_async_remote_copy(
            src_ref=src, dst_ref=dst, send_sem=ss, recv_sem=rs, device_id=dev, device_id_type=MESH
        )
        cp.start()
        pending.append(cp)

    def sib_send(ref, index):
        pltpu.make_async_remote_copy(
            src_ref=ref, dst_ref=ref, send_sem=sib_s.at[index], recv_sem=sib_r.at[index],
            device_id=sib, device_id_type=MESH,
        ).start()

    def arrive(dst, rs, ss):
        pltpu.make_async_remote_copy(
            src_ref=dst, dst_ref=dst, send_sem=ss, recv_sem=rs, device_id=sib, device_id_type=MESH
        ).wait_recv()

    def sib_wait(ref, index):
        pltpu.make_async_remote_copy(
            src_ref=ref, dst_ref=ref, send_sem=sib_s.at[index], recv_sem=sib_r.at[index],
            device_id=sib, device_id_type=MESH,
        ).wait()

    partners = [sib]
    partners += [at(dy=d) for d in range(1, NY)]
    partners += [at(dx=d) for d in range(1, NX)]
    partners += [at(dz=d) for d in range(1, NZ)]
    barrier = pltpu.get_barrier_semaphore()
    for p in partners:
        pl.semaphore_signal(barrier, inc=1, device_id=p, device_id_type=MESH)

    own = pl.ds(grp * 8, 8)
    loads = []

    def load(src, dst):
        cp = pltpu.make_async_copy(src, dst, load_sem.at[len(loads)])
        cp.start()
        loads.append(cp)
        return cp

    l_ft = load(features, GF.at[own])
    l_fs = load(fstore.at[pl.ds(2 * c, 2)], HF.at[z, x, pl.ds(2 * c, 2)])
    l_hs = load(hstore.at[pl.ds(2 * c, 2)], HH.at[z, x, pl.ds(2 * c, 2)])
    l_ta = load(gtiles, TA)
    l_tb = load(htiles, TB)
    l_ct = load(cot_h, COT)
    l_w = [load(s1_h, S1), load(n1_h, N1), load(s2_h, S2), load(n2_h, N2)]

    la, lb = 2 * c, 2 * c + 1
    LOW, HIGH = pl.ds(0, 64), pl.ds(64, 64)

    def zz(d):
        return (z + d) % NZ

    def xx(d):
        return (x + d) % NX

    def a_x1(X, n):
        r = X.at[z, x, la]
        send(r, r, axs.at[n, 0], axr.at[n, 0], at(dx=1))
        send(r, r, axs.at[n, 1], axr.at[n, 1], at(dx=-1))

    def a_x1_in(X, n):
        arrive(X.at[z, xx(-1), la], axr.at[n, 0], axs.at[n, 0])
        arrive(X.at[z, xx(1), la], axr.at[n, 1], axs.at[n, 1])

    def a_x2(X, n):
        r = X.at[z, xx(-1), la, LOW]
        send(r, r, axs.at[n, 2], axr.at[n, 2], at(dx=1))
        r = X.at[z, xx(1), la, HIGH]
        send(r, r, axs.at[n, 3], axr.at[n, 3], at(dx=-1))

    def a_x2_in(X, n):
        arrive(X.at[z, xx(2), la, LOW], axr.at[n, 2], axs.at[n, 2])
        arrive(X.at[z, xx(2), la, HIGH], axr.at[n, 3], axs.at[n, 3])

    def every_x(X, zi, l, part):
        return X.at[zi, pl.ds(0, NX), l] if part is None else X.at[zi, pl.ds(0, NX), l, part]

    def a_z(X, n, j):
        low, high = (LOW, HIGH) if j == 4 else (None, None)
        r = every_x(X, zz(-(j - 1)), la, low)
        send(r, r, azs.at[n, 2 * j - 2], azr.at[n, 2 * j - 2], at(dz=1))
        r = every_x(X, zz(j - 1), la, high)
        send(r, r, azs.at[n, 2 * j - 1], azr.at[n, 2 * j - 1], at(dz=-1))

    def a_z_in(X, n, j):
        low, high = (LOW, HIGH) if j == 4 else (None, None)
        arrive(every_x(X, zz(-j), la, low), azr.at[n, 2 * j - 2], azs.at[n, 2 * j - 2])
        arrive(every_x(X, zz(j), la, high), azr.at[n, 2 * j - 1], azs.at[n, 2 * j - 1])

    def one(X, zi, xi, l, part):
        return X.at[zi, xi, l] if part is None else X.at[zi, xi, l, part]

    def b_z(X, n, j):
        low, high = (LOW, HIGH) if j == 4 else (None, None)
        r = one(X, zz(-(j - 1)), x, lb, low)
        send(r, r, bzs.at[n, 2 * j - 2], bzr.at[n, 2 * j - 2], at(dz=1))
        r = one(X, zz(j - 1), x, lb, high)
        send(r, r, bzs.at[n, 2 * j - 1], bzr.at[n, 2 * j - 1], at(dz=-1))

    def b_z_in(X, n, j):
        low, high = (LOW, HIGH) if j == 4 else (None, None)
        arrive(one(X, zz(-j), x, lb, low), bzr.at[n, 2 * j - 2], bzs.at[n, 2 * j - 2])
        arrive(one(X, zz(j), x, lb, high), bzr.at[n, 2 * j - 1], bzs.at[n, 2 * j - 1])

    def b_x1(X, n, ds):
        for d in ds:
            r = X.at[zz(d), x, lb]
            e = d % NZ
            send(r, r, bxs.at[n, 4 * e], bxr.at[n, 4 * e], at(dx=1))
            send(r, r, bxs.at[n, 4 * e + 1], bxr.at[n, 4 * e + 1], at(dx=-1))

    def b_x1_in_x2(X, n, ds):
        for d in ds:
            e = d % NZ
            arrive(X.at[zz(d), xx(-1), lb], bxr.at[n, 4 * e], bxs.at[n, 4 * e])
            r = X.at[zz(d), xx(-1), lb, LOW]
            send(r, r, bxs.at[n, 4 * e + 2], bxr.at[n, 4 * e + 2], at(dx=1))
            arrive(X.at[zz(d), xx(1), lb], bxr.at[n, 4 * e + 1], bxs.at[n, 4 * e + 1])
            r = X.at[zz(d), xx(1), lb, HIGH]
            send(r, r, bxs.at[n, 4 * e + 3], bxr.at[n, 4 * e + 3], at(dx=-1))

    def b_x2_in(X, n, ds):
        for d in ds:
            e = d % NZ
            arrive(X.at[zz(d), xx(2), lb, LOW], bxr.at[n, 4 * e + 2], bxs.at[n, 4 * e + 2])
            arrive(X.at[zz(d), xx(2), lb, HIGH], bxr.at[n, 4 * e + 3], bxs.at[n, 4 * e + 3])
            sib_send(every_x(X, zz(d), lb, None), n)

    def a_share(X, n, ds):
        for d in ds:
            sib_send(every_x(X, zz(d), la, None), n)

    def plane(X, n, r):
        if r == 0:
            a_x1(X, n)
            b_z(X, n, 1)
            b_x1(X, n, (0,))
        elif r == 1:
            a_x1_in(X, n)
            a_x2(X, n)
            b_z_in(X, n, 1)
            b_z(X, n, 2)
            b_x1(X, n, (-1, 1))
            b_x1_in_x2(X, n, (0,))
        elif r == 2:
            a_x2_in(X, n)
            a_z(X, n, 1)
            b_z_in(X, n, 2)
            b_z(X, n, 3)
            b_x1(X, n, (-2, 2))
            b_x1_in_x2(X, n, (-1, 1))
            b_x2_in(X, n, (0,))
            a_share(X, n, (0,))
        elif r == 3:
            a_z_in(X, n, 1)
            a_z(X, n, 2)
            b_z_in(X, n, 3)
            b_z(X, n, 4)
            b_x1(X, n, (-3, 3))
            b_x1_in_x2(X, n, (-2, 2))
            b_x2_in(X, n, (-1, 1))
            a_share(X, n, (-1, 1))
        elif r == 4:
            b_z_in(X, n, 4)
            b_x1(X, n, (4,))
            a_z_in(X, n, 2)
            a_z(X, n, 3)
            b_x1_in_x2(X, n, (-3, 3))
            b_x2_in(X, n, (-2, 2))
            a_share(X, n, (-2, 2))
        elif r == 5:
            b_x1_in_x2(X, n, (4,))
            a_z_in(X, n, 3)
            a_z(X, n, 4)
            b_x2_in(X, n, (-3, 3))
            a_share(X, n, (-3, 3))
        else:
            b_x2_in(X, n, (4,))
            a_z_in(X, n, 4)
            a_share(X, n, (4,))

    def plane_done(X, n):
        sib_wait(X.at[:, :, pl.ds(2 * o, 2)], n)

    def chunk(X, d, first=0, many=8):
        return X.at[pl.ds((((y + d) % NY) * 2 + c) * 8 + first, many)]

    def ring(X, n, r):
        if r == 0:
            q = chunk(X, 0)
            send(q, q, ysem_s.at[n, 0], ysem_r.at[n, 0], at(dy=1))
            send(q, q, ysem_s.at[n, 1], ysem_r.at[n, 1], at(dy=-1))
            sib_send(q, 2 + n)
        elif r == 1:
            q = chunk(X, -1)
            arrive(q, ysem_r.at[n, 0], ysem_s.at[n, 0])
            h = chunk(X, -1, 0, 4)
            send(h, h, ysem_s.at[n, 2], ysem_r.at[n, 2], at(dy=1))
            sib_send(q, 2 + n)
            q = chunk(X, 1)
            arrive(q, ysem_r.at[n, 1], ysem_s.at[n, 1])
            h = chunk(X, 1, 4, 4)
            send(h, h, ysem_s.at[n, 3], ysem_r.at[n, 3], at(dy=-1))
            sib_send(q, 2 + n)
        else:
            arrive(chunk(X, 2, 0, 4), ysem_r.at[n, 2], ysem_s.at[n, 2])
            arrive(chunk(X, 2, 4, 4), ysem_r.at[n, 3], ysem_s.at[n, 3])
            sib_send(chunk(X, 2), 2 + n)

    def ring_done(X, n):
        sib_wait(X.at[pl.ds(0, 32)], 2 + n)

    l_fs.wait()
    l_ft.wait()
    l_hs.wait()
    pl.semaphore_wait(barrier, len(partners))
    plane(HF, 0, 0)
    ring(GF, 0, 0)
    plane(HH, 1, 0)
    l_ta.wait()
    l_tb.wait()
    l_ct.wait()

    @pl.loop(0, 8)
    def _(k):
        near_live, far_live = sc[7, k], sc[7, 8 + k]
        total = jnp.zeros((128, 128), F32)
        for s in range(8):
            t = TA[k * 8 + s].astype(F32) * jnp.where(s < near_live, 1.0, 0.0)
            TA[k * 8 + s] = t.astype(BF16)
            total = total + t
        for s in range(4):
            t = TB[k * 4 + s].astype(F32) * jnp.where(s < far_live, 1.0, 0.0)
            TB[k * 4 + s] = t.astype(BF16)
            total = total + t
        inv = 1.0 / (1.0 + jnp.sum(total, axis=1, keepdims=True))
        INV[k] = jnp.broadcast_to(inv, (128, 128))
        SC[k] = (COT[k].astype(F32) * inv).astype(BF16)

    plane(HF, 0, 1)

    def term(i, acc):
        acc = acc * sc[2, i].astype(F32) + dot_t(TA[sc[0, i]], SC[sc[1, i]])
        RT[i] = acc.astype(BF16)
        return acc

    acc = lax.fori_loop(0, 32, term, jnp.zeros((128, 256), F32))
    plane(HH, 1, 1)
    plane(HF, 0, 2)
    acc = lax.fori_loop(32, 64, term, acc)
    ring(GF, 0, 1)

    @pl.loop(0, 32)
    def _(i):
        g = ((i // 8) * 2 + o) * 8 + i % 8
        PS[i] = (RT[sc[3, g]].astype(F32) * sc[4, g].astype(F32)).astype(BF16)

    send(PS, PR, ps_s, ps_r, sib)
    plane(HF, 0, 3)
    plane(HH, 1, 2)
    ring(GF, 0, 2)
    arrive(PR, ps_r, ps_s)

    @pl.loop(0, 32)
    def _(i):
        g = ((i // 8) * 2 + c) * 8 + i % 8
        v = RT[sc[3, g]].astype(F32) * sc[4, g].astype(F32) + PR[i].astype(F32)
        Q[i] = v.astype(BF16)

    def piece(d, first):
        return Q.at[pl.ds(((y + d) % NY) * 8 + first, 4)]

    send(piece(2, 0), T1.at[0], rs_s.at[0], rs_r.at[0], at(dy=1))
    send(piece(2, 4), T1.at[1], rs_s.at[1], rs_r.at[1], at(dy=-1))
    send(piece(1, 4), FR.at[0, pl.ds(4, 4)], rs_s.at[2], rs_r.at[2], at(dy=1))
    send(piece(-1, 0), FR.at[1, pl.ds(0, 4)], rs_s.at[3], rs_r.at[3], at(dy=-1))
    plane(HF, 0, 4)
    ring_done(GF, 0)

    @pl.loop(0, 8)
    def _(k):
        total = jnp.zeros((128, 128), F32)
        for s in range(8):
            total = total + dot(TA[k * 8 + s], GF[sc[5, k * 8 + s]])
        ACC[k] = total

    plane(HF, 0, 5)
    plane(HH, 1, 3)
    for w in l_w:
        w.wait()
    plane(HF, 0, 6)
    plane_done(HF, 0)

    @pl.loop(0, 8)
    def _(k):
        total = ACC[k]
        for s in range(4):
            f = sc[6, k * 4 + s]
            total = total + dot(TB[k * 4 + s], HF[f // 16, (f // 4) % 4, f % 4])
        mean = (total * INV[k]).astype(BF16)
        GM[grp * 8 + k] = mean
        pre = dot(GF[grp * 8 + k], S1[...]) + dot(mean, N1[...])
        PRE[k] = pre
        HO[k] = (pre * jax.nn.sigmoid(pre)).astype(BF16)

    ring(GM, 1, 0)
    plane(HH, 1, 4)

    arrive(T1.at[0], rs_r.at[0], rs_s.at[0])

    @pl.loop(0, 4)
    def _(i):
        j = ((y + 1) % NY) * 8 + i
        Q[j] = (Q[j].astype(F32) + T1[0, i].astype(F32)).astype(BF16)

    send(piece(1, 0), FR.at[0, pl.ds(0, 4)], rs_s.at[4], rs_r.at[4], at(dy=1))
    arrive(T1.at[1], rs_r.at[1], rs_s.at[1])

    @pl.loop(0, 4)
    def _(i):
        j = ((y + 3) % NY) * 8 + 4 + i
        Q[j] = (Q[j].astype(F32) + T1[1, i].astype(F32)).astype(BF16)

    send(piece(-1, 4), FR.at[1, pl.ds(4, 4)], rs_s.at[5], rs_r.at[5], at(dy=-1))

    def put(first, rows, v):
        G[pl.ds(first, rows), :] = v[:, :128].astype(BF16)
        G[pl.ds(first + rows, rows), :] = v[:, 128:].astype(BF16)

    GP[...] = jnp.zeros_like(GP)

    @pl.loop(0, 8)
    def _(k):
        GP[...] = GP[...] + dot_t(HO[k], COT[k])

    put(512, 256, GP[...])
    plane(HH, 1, 5)
    ring(GM, 1, 1)
    plane(HH, 1, 6)
    plane_done(HH, 1)

    GP[...] = jnp.zeros_like(GP)

    @pl.loop(0, 8)
    def _(k):
        total = jnp.zeros((128, 256), F32)
        for s in range(4):
            f = sc[6, k * 4 + s]
            total = total + dot(TB[k * 4 + s], HH[f // 16, (f // 4) % 4, f % 4])
        FAR[k] = total
        inv = INV[k]
        m = jnp.concatenate([total[:, :128] * inv, total[:, 128:] * inv], axis=1).astype(BF16)
        GP[...] = GP[...] + dot_t(m, COT[k])

    ring(GM, 1, 2)
    arrive(FR.at[0, pl.ds(4, 4)], rs_r.at[2], rs_s.at[2])
    arrive(FR.at[1, pl.ds(0, 4)], rs_r.at[3], rs_s.at[3])
    arrive(FR.at[0, pl.ds(0, 4)], rs_r.at[4], rs_s.at[4])
    arrive(FR.at[1, pl.ds(4, 4)], rs_r.at[5], rs_s.at[5])

    MF[...] = jnp.zeros_like(MF)

    @pl.loop(0, 8)
    def _(k):
        r = Q[y * 8 + k].astype(F32) + FR[0, k].astype(F32) + FR[1, k].astype(F32)
        r = r.astype(BF16)
        GP[...] = GP[...] + dot_t(HO[k], r)
        total = dot_nt(COT[k], S2[...]) + dot_nt(r, N2[...])
        pre = PRE[k]
        sigma = jax.nn.sigmoid(pre)
        gp = (total * sigma * (1.0 + pre * (1.0 - sigma))).astype(BF16)
        MF[0] = MF[0] + dot_t(GF[grp * 8 + k], gp)
        MF[1] = MF[1] + dot_t(GM[grp * 8 + k], gp)

    put(1024, 256, GP[...])
    put(0, 128, MF[0])
    put(256, 128, MF[1])

    send(G.at[pl.ds(o * 768, 768)], B1, a_s.at[0], a_r.at[0], sib)
    ring_done(GM, 1)

    def group_hidden(first, many):
        @pl.loop(first, first + many)
        def _(j):
            pre = dot(GF[j], S1[...]) + dot(GM[j], N1[...])
            GH[j] = (pre * jax.nn.sigmoid(pre)).astype(BF16)

    arrive(B1, a_r.at[0], a_s.at[0])
    Q1[...] = (G[pl.ds(c * 768, 768), :].astype(F32) + B1[...].astype(F32)).astype(BF16)
    for d in range(1, NY):
        send(Q1.at[pl.ds(((y + d) % NY) * 192, 192)], B2.at[d - 1], b2s.at[d - 1], b2r.at[d - 1], at(dy=d))
    group_hidden(0, 32)
    for d in range(1, NY):
        arrive(B2.at[d - 1], b2r.at[d - 1], b2s.at[d - 1])
    Q2[...] = (
        Q1[pl.ds(y * 192, 192), :].astype(F32) + B2[0].astype(F32) + B2[1].astype(F32) + B2[2].astype(F32)
    ).astype(BF16)
    for d in range(1, NX):
        send(Q2.at[pl.ds(((x + d) % NX) * 48, 48)], B3.at[d - 1], b3s.at[d - 1], b3r.at[d - 1], at(dx=d))
    group_hidden(32, 32)
    for d in range(1, NX):
        arrive(B3.at[d - 1], b3r.at[d - 1], b3s.at[d - 1])
    B4[z] = (
        Q2[pl.ds(x * 48, 48), :].astype(F32) + B3[0].astype(F32) + B3[1].astype(F32) + B3[2].astype(F32)
    ).astype(BF16)
    for d in range(1, NZ):
        send(B4.at[z], B4.at[z], b4s.at[d - 1], b4r.at[d - 1], at(dz=d))

    @pl.loop(0, 8)
    def _(k):
        total = FAR[k]
        for s in range(8):
            total = total + dot(TA[k * 8 + s], GH[sc[5, k * 8 + s]])
        inv = INV[k]
        m = jnp.concatenate([total[:, :128] * inv, total[:, 128:] * inv], axis=1).astype(BF16)
        emb[k] = (dot(HO[k], S2[...]) + dot(m, N2[...])).astype(BF16)

    for d in range(1, NZ):
        arrive(B4.at[zz(-d)], b4r.at[d - 1], b4s.at[d - 1])
    total = B4[0].astype(F32)
    for i in range(1, NZ):
        total = total + B4[i].astype(F32)
    mine = pl.ds(c * 768 + y * 192 + x * 48, 48)
    FG[mine, :] = total.astype(BF16)
    for d in range(1, NX):
        send(FG.at[mine], FG.at[mine], b5s.at[d - 1], b5r.at[d - 1], at(dx=d))
    for d in range(1, NX):
        arrive(FG.at[pl.ds(c * 768 + y * 192 + xx(-d) * 48, 48)], b5r.at[d - 1], b5s.at[d - 1])
    row = FG.at[pl.ds(c * 768 + y * 192, 192)]
    for d in range(1, NY):
        send(row, row, b6s.at[d - 1], b6r.at[d - 1], at(dy=d))
    for d in range(1, NY):
        arrive(FG.at[pl.ds(c * 768 + ((y - d) % NY) * 192, 192)], b6r.at[d - 1], b6s.at[d - 1])
    half = FG.at[pl.ds(c * 768, 768)]
    send(half, half, a_s.at[1], a_r.at[1], sib)
    arrive(FG.at[pl.ds(o * 768, 768)], a_r.at[1], a_s.at[1])

    def take(first, rows, out):
        out[:, :128] = FG[pl.ds(first, rows), :].astype(F32)
        out[:, 128:] = FG[pl.ds(first + rows, rows), :].astype(F32)

    take(0, 128, gs1)
    take(256, 128, gn1)
    take(512, 256, gs2)
    take(1024, 256, gn2)
    for cp in pending:
        cp.wait_send()


def body(
    features, group_src, group_count, group_tiles, hist_owner, hist_local, hist_count, hist_tiles,
    feature_store, hidden_store, self_one, neigh_one, self_two, neigh_two, cotangent,
):
    scalars = prep(group_src, group_count, hist_owner, hist_local, hist_count)
    anywhere = pl.BlockSpec(memory_space=pl.ANY)
    vmem = pl.BlockSpec(memory_space=pltpu.VMEM)
    V, D, R = pltpu.VMEM, pltpu.SemaphoreType.DMA, pltpu.SemaphoreType.REGULAR
    scratch = [
        V((64, 128, 128), BF16), V((64, 128, 128), BF16), V((64, 128, 256), BF16),
        V((8, 4, 4, 128, 128), BF16), V((8, 4, 4, 128, 256), BF16),
        V((64, 128, 128), BF16), V((32, 128, 128), BF16), V((8, 128, 256), BF16),
        V((128, 256), BF16), V((128, 256), BF16), V((256, 256), BF16), V((256, 256), BF16),
        V((8, 128, 128), F32), V((8, 128, 256), BF16), V((64, 128, 256), BF16),
        V((32, 128, 256), BF16), V((32, 128, 256), BF16), V((32, 128, 256), BF16),
        V((2, 4, 128, 256), BF16), V((2, 8, 128, 256), BF16), V((8, 128, 256), BF16),
        V((8, 128, 128), F32), V((8, 128, 256), F32), V((8, 128, 256), BF16),
        V((8, 128, 256), F32), V((2, 128, 256), F32),
        V((1536, 128), BF16), V((256, 256), F32), V((768, 128), BF16), V((768, 128), BF16),
        V((3, 192, 128), BF16), V((192, 128), BF16), V((3, 48, 128), BF16), V((8, 48, 128), BF16),
        V((1536, 128), BF16),
        D((10,)), D((2, 4)), D((2, 4)), D((4,)), D((4,)),
        D((2, 4)), D((2, 4)), D((2, 8)), D((2, 8)), D((2, 8)), D((2, 8)), D((2, 32)), D((2, 32)),
        D((6,)), D((6,)), D, D, D((2,)), D((2,)),
        D((3,)), D((3,)), D((3,)), D((3,)), D((7,)), D((7,)), D((3,)), D((3,)), D((3,)), D((3,)),
    ]
    return pl.pallas_call(
        main_kernel,
        out_shape=(
            jax.ShapeDtypeStruct((8, 128, 256), BF16),
            jax.ShapeDtypeStruct((128, 256), F32),
            jax.ShapeDtypeStruct((128, 256), F32),
            jax.ShapeDtypeStruct((256, 256), F32),
            jax.ShapeDtypeStruct((256, 256), F32),
        ),
        in_specs=[pl.BlockSpec(memory_space=pltpu.SMEM)] + [anywhere] * 10,
        out_specs=(vmem,) * 5,
        scratch_shapes=scratch,
        compiler_params=pltpu.CompilerParams(
            collective_id=0, has_side_effects=True, vmem_limit_bytes=60 * 2**20
        ),
    )(
        scalars, features, group_tiles.reshape(64, 128, 128), hist_tiles.reshape(32, 128, 128),
        feature_store, hidden_store, self_one, neigh_one, self_two, neigh_two, cotangent,
    )


def solution(mesh):
    every = P(("grp", "wide"))
    wide = P("wide")
    placed = (every,) * 8 + (wide, wide) + (P(),) * 4 + (every,)
    return jax.shard_map(
        body, mesh=mesh, in_specs=placed, out_specs=(every, P(), P(), P(), P()), check_vma=False
    )
```

```python
import heapq

import jax
import jax.numpy as jnp
from jax import lax
from jax.experimental import pallas as pl
from jax.experimental.pallas import tpu as pltpu
from jax.sharding import PartitionSpec as P

MESH = pl.DeviceIdType.MESH
F32 = jnp.float32
BF16 = jnp.bfloat16
I32 = jnp.int32
NX, NY, NZ = 4, 4, 8
CUTS = (2, 4)


def dot(a, b):
    return jnp.dot(a, b, preferred_element_type=F32)


def dot_t(a, b):
    return lax.dot_general(a, b, (((0,), (0,)), ((), ())), preferred_element_type=F32)


def sigmoid(v):
    return 0.5 + 0.5 * jnp.tanh(0.5 * v)


class Plan:
    RATE = {"sib": 2.0}
    LATENCY = {"sib": 1000}
    AHEAD = 2000

    def __init__(self):
        self.now, self.count = 0.0, 0
        self.heap, self.jobs, self.done, self.busy, self.queue = [], [], set(), {}, {}

    def later(self, time, act):
        heapq.heappush(self.heap, (time, self.count, act))
        self.count += 1

    def transfer(self, link, kib, start, act, rank=0):
        queue = self.queue.setdefault(link, [])
        heapq.heappush(queue, (rank, self.count, kib, start, act))
        self.count += 1
        if len(queue) == 1:
            self.pump(link)

    def pump(self, link):
        queue = self.queue[link]
        while queue:
            free = self.busy.get(link, 0.0) - self.AHEAD
            if free > self.now:
                self.later(free, lambda: self.pump(link))
                return
            _, _, kib, start, act = heapq.heappop(queue)
            start()
            self.now += 40
            end = max(self.now, self.busy.get(link, 0.0)) + kib * self.RATE.get(link, 22.0)
            self.busy[link] = end
            self.later(end + self.LATENCY.get(link, 1500), act)

    def job(self, needs, cost, act, gives=None):
        self.jobs.append((set(needs), cost, act, gives))

    def mark(self, flag):
        self.done.add(flag)

    def run(self):
        while self.heap or self.jobs:
            if self.heap and self.heap[0][0] <= self.now:
                self.now += 30
                heapq.heappop(self.heap)[2]()
                continue
            ready = [j for j in self.jobs if j[0] <= self.done]
            if ready:
                job = ready[0]
                self.jobs.remove(job)
                job[2]()
                self.now += job[1]
                if job[3] is not None:
                    self.done.add(job[3])
            else:
                self.now = self.heap[0][0]


def main_kernel(
    gsrc, gcnt, howner, hlocal, hcnt, features, gtiles, htiles, fstore, hstore, s1_h, n1_h, s2_h, n2_h, cot_h,
    emb, grads,
    GF, GM, GH, HF, HH, TA, TB, COT, W1, W2, W2T,
    INV, SCT, RT, PS, PR, Q, T1, FR, RB, ACC, PRE, HO, FAR, MF, GP,
    G, B1, Q1, B2, B4, FG, TBV, TBS,
    load_sem, tb_sem, sib_s, sib_r, pl_s, az_r, ax_r, bz_r, bx_r, y_s, y_r, rs_s, rs_r, ps_s, ps_r,
    a_s, a_r, b2s, b2r, b4s, b4r, b5s, b5r,
):
    grp = lax.axis_index("grp")
    wide = lax.axis_index("wide")
    z, x = wide // NX, wide % NX
    y, c = grp // 2, grp % 2
    o = 1 - c
    plan = Plan()

    def zz(d):
        return (z + d) % NZ

    def xx(d):
        return (x + d) % NX

    def yy(d):
        return (y + d) % NY

    def at(dz=0, dy=0, dx=0):
        return (yy(dy) * 2 + c, zz(dz) * NX + xx(dx))

    sib = (y * 2 + o, wide)
    STEP = {"x+": at(dx=1), "x-": at(dx=-1), "y+": at(dy=1), "y-": at(dy=-1), "z+": at(dz=1), "z-": at(dz=-1)}

    def remote(src, dst, ss, rs, dev):
        return pltpu.make_async_remote_copy(
            src_ref=src, dst_ref=dst, send_sem=ss, recv_sem=rs, device_id=dev, device_id_type=MESH
        )

    def push(link, kib, src, dst, arrives, ss, rs, then, rank):
        def arrived():
            remote(arrives, arrives, ss, rs, sib).wait_recv()
            then()

        plan.transfer(link, kib, remote(src, dst, ss, rs, STEP[link]).start, arrived, rank)

    partners = [sib]
    partners += [at(dy=dy, dx=dx) for dy in range(NY) for dx in range(NX) if (dy, dx) != (0, 0)]
    partners += [at(dz=d) for d in range(1, NZ)]
    barrier = pltpu.get_barrier_semaphore()
    for p in partners:
        pl.semaphore_signal(barrier, inc=1, device_id=p, device_id_type=MESH)

    loads = []

    def load(src, dst):
        cp = pltpu.make_async_copy(src, dst, load_sem.at[len(loads)])
        cp.start()
        loads.append(cp)
        return cp

    l_fs = load(fstore.at[c], HF.at[z, x, c])
    l_ft = load(features, GF.at[pl.ds(grp * 8, 8)])
    l_hs = load(hstore.at[c], HH.at[z, x, c])
    l_ta = load(gtiles, TA)
    l_tb = load(htiles, TB)
    l_ct = load(cot_h, COT)
    l_w = [
        load(s1_h, W1.at[pl.ds(0, 128)]), load(n1_h, W1.at[pl.ds(128, 128)]),
        load(s2_h, W2.at[pl.ds(0, 256)]), load(n2_h, W2.at[pl.ds(256, 256)]),
    ]

    lane = lax.broadcasted_iota(I32, (8, 128), 1)
    sources = [gsrc[i // 8, i % 8] for i in range(64)]
    named_row = jnp.zeros((8, 128), I32)
    for i, s in enumerate(sources):
        named_row = jnp.where(lane == i, s, named_row)
    place = jnp.zeros((8, 128), I32)
    upto = jnp.zeros((8, 128), I32)
    many = jnp.zeros((8, 128), I32)
    for i, s in enumerate(sources):
        place = place + jnp.where((s < named_row) | ((s == named_row) & (lane > i)), 1, 0)
        upto = upto + jnp.where(lane >= s, 1, 0)
        many = many + jnp.where(lane == s, 1, 0)
    place_col = jnp.transpose(jnp.broadcast_to(place[0:1], (128, 128)))[:64]
    named_col = jnp.transpose(jnp.broadcast_to(named_row[0:1], (128, 128)))[:64]
    hit = place_col == lax.broadcasted_iota(I32, (64, 128), 1)
    order = jnp.sum(jnp.where(hit, lax.broadcasted_iota(I32, (64, 128), 0), 0), axis=0, keepdims=True)
    target = jnp.sum(jnp.where(hit, named_col, 0), axis=0, keepdims=True)
    target = jnp.broadcast_to(target, (8, 128))
    same = jnp.where((target == pltpu.roll(target, 1, 1)) & (lane > 0), 1, 0)
    TBV[0:1, :] = order
    TBV[1:2, :] = order >> 3
    TBV[2:3, :] = same[0:1]
    TBV[3:4, :] = jnp.maximum(upto - 1, 0)[0:1]
    TBV[4:5, :] = jnp.minimum(many, 1)[0:1]
    l_tbl = pltpu.make_async_copy(TBV, TBS, tb_sem)
    l_tbl.start()

    class Plane:
        def __init__(self, X, n, unit, flag):
            self.X, self.n, self.unit, self.flag = X, n, unit, flag
            cut = CUTS[n]
            self.rows = {"a": (0, cut), "b": (cut, 8 - cut)}
            self.left = 16

        def at(self, zi, xi, kind, part=None):
            first, rows = self.rows[kind]
            if part is not None:
                rows = rows // 2
                first = first + part * rows
            return self.X.at[zi, xi, c, pl.ds(first, rows)]

        def kib(self, kind, part):
            return self.rows[kind][1] * self.unit / (1 if part is None else 2)

        def go(self, link, zi, xi, arrive, kind, part, rs, then):
            r = self.at(zi, xi, kind, part)
            rank = 2 * self.n + int((kind == "a") == (link[0] == "z"))
            push(link, self.kib(kind, part), r, r, self.at(*arrive, kind, part), pl_s.at[self.n], rs, then, rank)

        def share(self, zi, kind):
            first, rows = self.rows[kind]
            r = self.X.at[zi, pl.ds(0, NX), c, pl.ds(first, rows)]
            self.left -= 1
            act = self.finish if self.left == 0 else lambda: None
            copy = remote(r, r, sib_s.at[self.n], sib_r.at[self.n], sib)
            plan.transfer("sib", 4 * self.kib(kind, None), copy.start, act)

        def finish(self):
            r = self.X.at[:, :, o]
            remote(r, r, sib_s.at[self.n], sib_r.at[self.n], sib).wait()
            plan.mark(self.flag)

        def x_ring(self, kind, d, sem, have, whole):
            n, state = self.n, {"halves": 0, "units": 1}

            def unit(dx):
                have(dx)
                state["units"] += 1
                if state["units"] == 4:
                    whole()

            def half():
                state["halves"] += 1
                if state["halves"] == 2:
                    unit(2)

            def first(s):
                def then():
                    link, part = ("x+", 0) if s == 1 else ("x-", 1)
                    self.go(link, zz(d), xx(-s), (zz(d), xx(2)), kind, part, sem(2 + part), half)
                    unit(-s)

                return then

            self.go("x+", zz(d), x, (zz(d), xx(-1)), kind, None, sem(0), first(1))
            self.go("x-", zz(d), x, (zz(d), xx(1)), kind, None, sem(1), first(-1))

        def z_ring(self, kind, dx, sem, have, whole):
            state = {"halves": 0}

            def half():
                state["halves"] += 1
                if state["halves"] == 2:
                    have(4)

            def hop(s, j):
                link = "z+" if s == 1 else "z-"
                part = None if j < 4 else (0 if s == 1 else 1)

                def then():
                    if j == 4:
                        half()
                        return
                    hop(s, j + 1)
                    have(-s * j)

                index = 2 * (j - 1) + (0 if s == 1 else 1)
                self.go(link, zz(-s * (j - 1)), xx(dx), (zz(-s * j), xx(dx)), kind, part, sem(index), then)

            hop(1, 1)
            hop(-1, 1)

        def start(self):
            n = self.n
            rows_a = {}

            def have_a(dz):
                rows_a[dz % NZ] = rows_a.get(dz % NZ, 0) + 1
                if rows_a[dz % NZ] == 4:
                    self.share(zz(dz), "a")

            def a_unit(dx):
                have_a(0)
                base = 8 * (dx % NX)
                self.z_ring("a", dx, lambda i: az_r.at[n, base + i], have_a, None)

            def b_unit(dz):
                base = 4 * (dz % NZ)
                self.x_ring(
                    "b", dz, lambda i: bx_r.at[n, base + i], lambda dx: None, lambda: self.share(zz(dz), "b")
                )

            self.z_ring("b", 0, lambda i: bz_r.at[n, i], b_unit, None)
            self.x_ring("a", 0, lambda i: ax_r.at[n, i], a_unit, lambda: None)
            b_unit(0)
            a_unit(0)

    class Ring:
        def __init__(self, X, n, flag):
            self.X, self.n, self.flag, self.left = X, n, flag, 7

        def at(self, d, part):
            return self.X.at[pl.ds((yy(d) * 2 + c) * 8 + 4 * part, 4)]

        def go(self, s, d, part, index, then):
            link = "y+" if s == 1 else "y-"
            r = self.at(d, part)
            push(link, 128, r, r, self.at(d - s, part), y_s.at[self.n], y_r.at[self.n, index], then, 2 * self.n)

        def share(self, d, part=None):
            r = self.X.at[pl.ds((yy(d) * 2 + c) * 8, 8)] if part is None else self.at(d, part)
            self.left -= 1
            act = self.finish if self.left == 0 else lambda: None
            copy = remote(r, r, sib_s.at[2 + self.n], sib_r.at[2 + self.n], sib)
            plan.transfer("sib", 128, copy.start, act)

        def finish(self):
            r = self.X.at[pl.ds(0, 32)]
            remote(r, r, sib_s.at[2 + self.n], sib_r.at[2 + self.n], sib).wait()
            plan.mark(self.flag)

        def start(self):
            def lead(s, part):
                def then():
                    self.go(s, -s, part, 4 + part, lambda: self.share(2, part))
                    self.share(-s, part)

                return then

            self.go(1, 0, 0, 0, lead(1, 0))
            self.go(-1, 0, 1, 1, lead(-1, 1))
            self.go(1, 0, 1, 2, lambda: self.share(-1, 1))
            self.go(-1, 0, 0, 3, lambda: self.share(1, 0))
            self.share(0)

    def degrees(first, many):
        def act():
            @pl.loop(first, first + many)
            def _(k):
                near_live, far_live = gcnt[k], hcnt[k]
                total = jnp.zeros((128, 128), F32)
                for s in range(8):
                    t = TA[k * 8 + s].astype(F32) * jnp.where(s < near_live, 1.0, 0.0)
                    TA[k * 8 + s] = t.astype(BF16)
                    total = total + t
                for s in range(4):
                    t = TB[k * 4 + s].astype(F32) * jnp.where(s < far_live, 1.0, 0.0)
                    TB[k * 4 + s] = t.astype(BF16)
                    total = total + t
                inv = 1.0 / (1.0 + jnp.sum(total, axis=1, keepdims=True))
                INV[k] = jnp.broadcast_to(inv, (128, 128))
                SCT[k] = jnp.transpose(COT[k].astype(F32) * inv).astype(BF16)

        return act

    held = {}

    def terms(first, many):
        def term(i, acc):
            acc = acc * TBS[2, i].astype(F32) + dot(SCT[TBS[1, i]], TA[TBS[0, i]])
            RT[i] = acc.astype(BF16)
            return acc

        def act():
            start = held.get("acc")
            start = jnp.zeros((256, 128), F32) if start is None else start
            held["acc"] = lax.fori_loop(first, first + many, term, start, unroll=4)

        return act

    def partial(g):
        return RT[TBS[3, g]].astype(F32) * TBS[4, g].astype(F32)

    def for_sibling(d):
        def act():
            @pl.loop(0, 8)
            def _(i):
                PS[yy(d) * 8 + i] = partial((yy(d) * 2 + o) * 8 + i).astype(BF16)

            r = pl.ds(yy(d) * 8, 8)
            copy = remote(PS.at[r], PR.at[r], ps_s, ps_r.at[d], sib)

            def then():
                copy.wait_recv()
                plan.mark(f"PR{d}")

            plan.transfer("sib", 512, copy.start, then, -1)

        return act

    def piece(d, part):
        return Q.at[pl.ds(yy(d) * 8 + 4 * part, 4)]

    def back(link, src, dst, index, then):
        push(link, 256, src, dst, dst, rs_s, rs_r.at[index], then, 1)

    def combine(d):
        def act():
            @pl.loop(0, 8)
            def _(i):
                g = (yy(d) * 2 + c) * 8 + i
                Q[yy(d) * 8 + i] = (partial(g) + PR[yy(d) * 8 + i].astype(F32)).astype(BF16)

            if d == 2:
                back("y+", piece(2, 0), T1.at[0], 0, lambda: plan.mark("T0"))
                back("y-", piece(2, 1), T1.at[1], 1, lambda: plan.mark("T1"))
            elif d == 1:
                back("y+", piece(1, 1), FR.at[0, pl.ds(4, 4)], 2, lambda: plan.mark("R2"))
            elif d == 3:
                back("y-", piece(-1, 0), FR.at[1, pl.ds(0, 4)], 3, lambda: plan.mark("R3"))

        return act

    def onward(part):
        def act():
            d = 1 if part == 0 else -1

            @pl.loop(0, 4)
            def _(i):
                j = yy(d) * 8 + 4 * part + i
                Q[j] = (Q[j].astype(F32) + T1[part, i].astype(F32)).astype(BF16)

            link = "y+" if part == 0 else "y-"
            flag = "R4" if part == 0 else "R5"
            back(link, piece(d, part), FR.at[part, pl.ds(4 * part, 4)], 4 + part, lambda: plan.mark(flag))

        return act

    def near_one(first, many):
        def act():
            @pl.loop(first, first + many)
            def _(k):
                total = jnp.zeros((128, 128), F32)
                for s in range(8):
                    total = total + dot(TA[k * 8 + s], GF[gsrc[k, s]])
                ACC[k] = total

        return act

    def far_of(X, k, s):
        w, l = howner[s, 0, k], hlocal[s, k]
        first = (l % 2) * 4
        return jnp.concatenate([X[w // 4, w % 4, l // 2, first + i] for i in range(4)], axis=0)

    def far_one():
        for w in l_w:
            w.wait()

        @pl.loop(0, 8)
        def _(k):
            total = ACC[k]
            for s in range(4):
                total = total + dot(TB[k * 4 + s], far_of(HF, k, s))
            mean = (total * INV[k]).astype(BF16)
            GM[grp * 8 + k] = mean
            pre = dot(jnp.concatenate([GF[grp * 8 + k], mean], axis=1), W1[...])
            PRE[k] = pre
            HO[k] = (pre * sigmoid(pre)).astype(BF16)

        Ring(GM, 1, "GM").start()

    def turned():
        W2T[pl.ds(0, 256), :] = jnp.transpose(W2[pl.ds(0, 256), :].astype(F32)).astype(BF16)
        W2T[pl.ds(256, 256), :] = jnp.transpose(W2[pl.ds(256, 256), :].astype(F32)).astype(BF16)

    def scaled(total, inv):
        return jnp.concatenate([total[:, :128] * inv, total[:, 128:] * inv], axis=1).astype(BF16)

    def far_two(first, many):
        def act():
            @pl.loop(first, first + many)
            def _(k):
                total = jnp.zeros((128, 256), F32)
                for s in range(4):
                    total = total + dot(TB[k * 4 + s], far_of(HH, k, s))
                FAR[k] = total
                MF[k] = scaled(total, INV[k])

        return act

    def returned():
        @pl.loop(0, 8)
        def _(k):
            r = Q[y * 8 + k].astype(F32) + FR[0, k].astype(F32) + FR[1, k].astype(F32)
            r = jnp.transpose(r).astype(BF16)
            RB[k] = r
            total = dot(jnp.concatenate([COT[k], r], axis=1), W2T[...])
            pre = PRE[k]
            sigma = sigmoid(pre)
            GP[k] = (total * sigma * (1.0 + pre * (1.0 - sigma))).astype(BF16)

    def flat(X):
        return X[...].reshape(1024, 256)

    def put(first, rows, v):
        G[pl.ds(first, rows), :] = v[:, :128].astype(BF16)
        G[pl.ds(first + rows, rows), :] = v[:, 128:].astype(BF16)

    def gradients_one():
        own = pl.ds(grp * 8, 8)
        both = jnp.concatenate([GF[own].reshape(1024, 128), GM[own].reshape(1024, 128)], axis=1)
        v = dot_t(both, flat(GP))
        put(0, 128, v[:128])
        put(256, 128, v[128:])

    def gradient_self_two():
        put(512, 256, dot_t(flat(HO), flat(COT)))

    def gradient_neigh_two():
        put(1024, 256, dot_t(flat(HO), flat(RB)) + dot_t(flat(MF), flat(COT)))

    def wait_all(copies, flag):
        def then():
            for cp in copies:
                cp.wait_recv()
            plan.mark(flag)

        return then

    waiting = []

    def exchange(copies, cost, flag, link="all"):
        for src, dst, ss, rs, dev, arrives in copies:
            cp = remote(src, dst, ss, rs, dev)
            cp.start()
            waiting.append(cp)
        plan.now += 40 * len(copies)
        plan.later(plan.now + cost, wait_all([remote(a, a, ss, rs, dev) for _, _, ss, rs, dev, a in copies], flag))

    def reduce_sib():
        exchange([(G.at[pl.ds(o * 768, 768)], B1, a_s.at[0], a_r.at[0], sib, B1)], 1500, "B1")

    around = [(dy, dx) for dy in range(NY) for dx in range(NX) if (dy, dx) != (0, 0)]

    def reduce_xy():
        Q1[...] = (G[pl.ds(c * 768, 768), :].astype(F32) + B1[...].astype(F32)).astype(BF16)
        exchange(
            [
                (
                    Q1.at[pl.ds(yy(dy) * 192 + xx(dx) * 48, 48)], B2.at[i], b2s.at[i], b2r.at[i],
                    at(dy=dy, dx=dx), B2.at[i],
                )
                for i, (dy, dx) in enumerate(around)
            ],
            5500, "B2",
        )

    def reduce_z():
        total = Q1[pl.ds(y * 192 + x * 48, 48), :].astype(F32)
        for i in range(15):
            total = total + B2[i].astype(F32)
        B4[z] = total.astype(BF16)
        exchange(
            [
                (B4.at[z], B4.at[z], b4s.at[d - 1], b4r.at[d - 1], at(dz=d), B4.at[zz(-d)])
                for d in range(1, NZ)
            ],
            5000, "B4",
        )

    def rows(dy, dx):
        return FG.at[pl.ds(c * 768 + yy(dy) * 192 + xx(dx) * 48, 48)]

    def gather_xy():
        total = B4[0].astype(F32)
        for i in range(1, NZ):
            total = total + B4[i].astype(F32)
        FG[pl.ds(c * 768 + y * 192 + x * 48, 48), :] = total.astype(BF16)
        exchange(
            [
                (rows(0, 0), rows(0, 0), b5s.at[i], b5r.at[i], at(dy=dy, dx=dx), rows(-dy, -dx))
                for i, (dy, dx) in enumerate(around)
            ],
            5500, "B5",
        )

    def gather_sib():
        mine, other = FG.at[pl.ds(c * 768, 768)], FG.at[pl.ds(o * 768, 768)]
        exchange([(mine, mine, a_s.at[1], a_r.at[1], sib, other)], 1500, "FG")

    def group_hidden(first, many):
        def act():
            @pl.loop(first // 2, (first + many) // 2)
            def _(j):
                two = pl.ds(j * 2, 2)
                both = jnp.concatenate([GF[two].reshape(256, 128), GM[two].reshape(256, 128)], axis=1)
                pre = dot(both, W1[...])
                GH[two] = (pre * sigmoid(pre)).astype(BF16).reshape(2, 128, 256)

        return act

    def near_two(first, many):
        def act():
            @pl.loop(first, first + many)
            def _(k):
                total = FAR[k]
                for s in range(8):
                    total = total + dot(TA[k * 8 + s], GH[gsrc[k, s]])
                m = scaled(total, INV[k])
                emb[k] = dot(jnp.concatenate([HO[k], m], axis=1), W2[...]).astype(BF16)

        return act

    def start():
        l_fs.wait()
        l_ft.wait()
        pl.semaphore_wait(barrier, len(partners))
        Plane(HF, 0, 8, "HF").start()
        Ring(GF, 0, "GF").start()

        def second():
            l_hs.wait()
            Plane(HH, 1, 16, "HH").start()

        plan.later(plan.now + 300, second)

    def first_wait():
        l_ta.wait()
        l_tb.wait()
        l_ct.wait()

    start()
    plan.job(["FG"], 100, lambda: None, "end")
    plan.job(["B5"], 100, gather_sib)
    plan.job(["B4"], 200, gather_xy)
    plan.job(["B2"], 200, reduce_z)
    plan.job(["B1"], 300, reduce_xy)
    plan.job(["g1", "gs2", "gn2"], 100, reduce_sib)
    plan.job([], 50, first_wait, "in")
    plan.job(["in"], 800, degrees(0, 4), "d0")
    plan.job(["d0"], 800, degrees(4, 4), "deg")
    plan.job(["HF", "n1"], 3000, far_one, "own")
    plan.job(["deg"], 50, l_tbl.wait, "tbl")
    for i in range(4):
        plan.job([f"t{i - 1}" if i else "tbl"], 1000, terms(16 * i, 16), f"t{i}")
    for d in (2, 1, 3, 0):
        plan.job(["t3"], 150, for_sibling(d))
    for d in (2, 1, 3, 0):
        plan.job([f"PR{d}"], 300, combine(d), f"q{d}")
    plan.job(["T0", "q1"], 200, onward(0))
    plan.job(["T1", "q3"], 200, onward(1))
    plan.job(["GF", "deg"], 900, near_one(0, 4), "n0")
    plan.job(["n0"], 900, near_one(4, 4), "n1")
    plan.job(["own"], 300, turned, "W2T")
    plan.job(["R2", "R3", "R4", "R5", "q0", "W2T"], 2200, returned, "RB")
    plan.job(["RB"], 900, gradients_one, "g1")
    plan.job(["HH"], 1000, far_two(0, 4), "f0")
    plan.job(["f0"], 1000, far_two(4, 4), "f1")
    plan.job(["RB", "f1"], 1500, gradient_neigh_two, "gn2")
    plan.job(["own"], 900, gradient_self_two, "gs2")
    for i in range(8):
        plan.job([f"h{i - 1}" if i else "GM", "own"], 700, group_hidden(8 * i, 8), f"h{i}")
    for i in range(4):
        plan.job([f"e{i - 1}" if i else "h7", "f1"], 1200, near_two(2 * i, 2), f"e{i}")
    plan.run()

    grads[...] = FG[...]
    for n in range(2):
        X = (GF, GH)[n].at[pl.ds(0, 62)]
        remote(X, X, pl_s.at[n], az_r.at[n, 0], sib).wait_send()
        X = GF.at[pl.ds(0, 24)]
        remote(X, X, y_s.at[n], y_r.at[n, 0], sib).wait_send()
    X = Q.at[pl.ds(0, 24)]
    remote(X, X, rs_s, rs_r.at[0], sib).wait_send()
    remote(PS, PR, ps_s, ps_r.at[0], sib).wait_send()
    for cp in waiting:
        cp.wait_send()


def last_kernel(emb_in, grads, emb, gs1, gn1, gs2, gn2):
    emb[...] = emb_in[...]

    def take(first, rows, out):
        out[:, :128] = grads[pl.ds(first, rows), :].astype(F32)
        out[:, 128:] = grads[pl.ds(first + rows, rows), :].astype(F32)

    take(0, 128, gs1)
    take(256, 128, gn1)
    take(512, 256, gs2)
    take(1024, 256, gn2)


def body(
    features, group_src, group_count, group_tiles, hist_owner, hist_local, hist_count, hist_tiles,
    feature_store, hidden_store, self_one, neigh_one, self_two, neigh_two, cotangent,
):
    anywhere = pl.BlockSpec(memory_space=pl.ANY)
    vmem = pl.BlockSpec(memory_space=pltpu.VMEM)
    smem = pl.BlockSpec(memory_space=pltpu.SMEM)
    V, D = pltpu.VMEM, pltpu.SemaphoreType.DMA
    scratch = [
        V((64, 128, 128), BF16), V((64, 128, 128), BF16), V((64, 128, 256), BF16),
        V((8, 4, 2, 8, 32, 128), BF16), V((8, 4, 2, 8, 32, 256), BF16),
        V((64, 128, 128), BF16), V((32, 128, 128), BF16), V((8, 128, 256), BF16),
        V((256, 256), BF16), V((512, 256), BF16), V((512, 256), BF16),
        V((8, 128, 128), F32), V((8, 256, 128), BF16), V((64, 256, 128), BF16),
        V((32, 256, 128), BF16), V((32, 256, 128), BF16), V((32, 256, 128), BF16),
        V((2, 4, 256, 128), BF16), V((2, 8, 256, 128), BF16), V((8, 128, 256), BF16),
        V((8, 128, 128), F32), V((8, 128, 256), F32), V((8, 128, 256), BF16),
        V((8, 128, 256), F32), V((8, 128, 256), BF16), V((8, 128, 256), BF16),
        V((1536, 128), BF16), V((768, 128), BF16), V((768, 128), BF16),
        V((15, 48, 128), BF16), V((8, 48, 128), BF16),
        V((1536, 128), BF16), V((8, 128), I32), pltpu.SMEM((8, 128), I32),
        D((12,)), D, D((4,)), D((4,)), D((2,)),
        D((2, 32)), D((2, 4)), D((2, 8)), D((2, 32)), D((2,)), D((2, 6)), D, D((6,)), D, D((4,)),
        D((2,)), D((2,)), D((15,)), D((15,)), D((7,)), D((7,)), D((15,)), D((15,)),
    ]
    emb, grads = pl.pallas_call(
        main_kernel,
        out_shape=(jax.ShapeDtypeStruct((8, 128, 256), BF16), jax.ShapeDtypeStruct((1536, 128), BF16)),
        in_specs=[smem] * 5 + [anywhere] * 10,
        out_specs=(vmem, vmem),
        scratch_shapes=scratch,
        compiler_params=pltpu.CompilerParams(
            collective_id=0, has_side_effects=True, vmem_limit_bytes=60 * 2**20
        ),
    )(
        group_src, group_count, hist_owner.transpose(1, 2, 0), hist_local.T, hist_count,
        features, group_tiles.reshape(64, 128, 128), hist_tiles.reshape(32, 128, 128),
        feature_store.reshape(2, 8, 32, 128), hidden_store.reshape(2, 8, 32, 256),
        self_one, neigh_one, self_two, neigh_two, cotangent,
    )
    return pl.pallas_call(
        last_kernel,
        out_shape=(
            jax.ShapeDtypeStruct((8, 128, 256), BF16),
            jax.ShapeDtypeStruct((128, 256), F32),
            jax.ShapeDtypeStruct((128, 256), F32),
            jax.ShapeDtypeStruct((256, 256), F32),
            jax.ShapeDtypeStruct((256, 256), F32),
        ),
        in_specs=[vmem] * 2,
        out_specs=(vmem,) * 5,
    )(emb, grads)


def solution(mesh):
    every = P(("grp", "wide"))
    wide = P("wide")
    placed = (every,) * 8 + (wide, wide) + (P(),) * 4 + (every,)
    return jax.shard_map(
        body, mesh=mesh, in_specs=placed, out_specs=(every, P(), P(), P(), P()), check_vma=False
    )
```

```python
import heapq

import jax
import jax.numpy as jnp
from jax import lax
from jax.experimental import pallas as pl
from jax.experimental.pallas import tpu as pltpu
from jax.sharding import PartitionSpec as P

MESH = pl.DeviceIdType.MESH
F32 = jnp.float32
BF16 = jnp.bfloat16
I32 = jnp.int32
NX, NY, NZ = 4, 4, 8
CUTS = (2, 4)


def dot(a, b):
    return jnp.dot(a, b, preferred_element_type=F32)


def dot_t(a, b):
    return lax.dot_general(a, b, (((0,), (0,)), ((), ())), preferred_element_type=F32)


def sigmoid(v):
    return 0.5 + 0.5 * jnp.tanh(0.5 * v)


class Plan:
    RATE = {"sib": 2.0}
    LATENCY = {"sib": 1000}
    AHEAD = 2000

    def __init__(self):
        self.now, self.count = 0.0, 0
        self.heap, self.jobs, self.done, self.busy, self.queue = [], [], set(), {}, {}

    def later(self, time, act):
        heapq.heappush(self.heap, (time, self.count, act))
        self.count += 1

    def transfer(self, link, kib, start, act, rank=0):
        queue = self.queue.setdefault(link, [])
        heapq.heappush(queue, (rank, self.count, kib, start, act))
        self.count += 1
        if len(queue) == 1:
            self.pump(link)

    def pump(self, link):
        queue = self.queue[link]
        while queue:
            free = self.busy.get(link, 0.0) - self.AHEAD
            if free > self.now:
                self.later(free, lambda: self.pump(link))
                return
            _, _, kib, start, act = heapq.heappop(queue)
            start()
            self.now += 15
            end = max(self.now, self.busy.get(link, 0.0)) + kib * self.RATE.get(link, 22.0)
            self.busy[link] = end
            self.later(end + self.LATENCY.get(link, 1500), act)

    def job(self, needs, cost, act, gives=None):
        self.jobs.append((set(needs), cost, act, gives))

    def mark(self, flag):
        self.done.add(flag)

    def run(self):
        while self.heap or self.jobs:
            if self.heap and self.heap[0][0] <= self.now:
                self.now += 15
                heapq.heappop(self.heap)[2]()
                continue
            ready = [j for j in self.jobs if j[0] <= self.done]
            if ready:
                job = ready[0]
                self.jobs.remove(job)
                job[2]()
                self.now += job[1]
                if job[3] is not None:
                    self.done.add(job[3])
            else:
                self.now = self.heap[0][0]


def main_kernel(
    gsrc, gcnt, howner, hlocal, hcnt, features, gtiles, htiles, fstore, hstore, s1_h, n1_h, s2_h, n2_h, cot_h,
    emb, grads,
    GF, GM, GH, HF, HH, TA, TB, COT, W1, W2, W2T,
    INV, SCT, RT, PS, PR, Q, T1, FR, RB, ACC, PRE, FAR, MF, GP,
    G, B1, Q1, B2, B4, FG, TBV, TBS,
    load_sem, tb_sem, sib_s, sib_r, pl_s, az_r, ax_r, bz_r, bx_r, y_s, y_r, rs_s, rs_r, ps_s, ps_r,
    a_s, a_r, b2s, b2r, b4s, b4r, b5s, b5r,
):
    grp = lax.axis_index("grp")
    wide = lax.axis_index("wide")
    z, x = wide // NX, wide % NX
    y, c = grp // 2, grp % 2
    o = 1 - c
    plan = Plan()

    def zz(d):
        return (z + d) % NZ

    def xx(d):
        return (x + d) % NX

    def yy(d):
        return (y + d) % NY

    def at(dz=0, dy=0, dx=0):
        return (yy(dy) * 2 + c, zz(dz) * NX + xx(dx))

    sib = (y * 2 + o, wide)
    STEP = {"x+": at(dx=1), "x-": at(dx=-1), "y+": at(dy=1), "y-": at(dy=-1), "z+": at(dz=1), "z-": at(dz=-1)}

    def remote(src, dst, ss, rs, dev):
        return pltpu.make_async_remote_copy(
            src_ref=src, dst_ref=dst, send_sem=ss, recv_sem=rs, device_id=dev, device_id_type=MESH
        )

    def push(link, kib, src, dst, arrives, ss, rs, then, rank):
        def arrived():
            remote(arrives, arrives, ss, rs, sib).wait_recv()
            then()

        plan.transfer(link, kib, remote(src, dst, ss, rs, STEP[link]).start, arrived, rank)

    partners = [sib]
    partners += [at(dy=dy, dx=dx) for dy in range(NY) for dx in range(NX) if (dy, dx) != (0, 0)]
    partners += [at(dz=d) for d in range(1, NZ)]
    barrier = pltpu.get_barrier_semaphore()
    for p in partners:
        pl.semaphore_signal(barrier, inc=1, device_id=p, device_id_type=MESH)

    loads = []

    def load(src, dst):
        cp = pltpu.make_async_copy(src, dst, load_sem.at[len(loads)])
        cp.start()
        loads.append(cp)
        return cp

    l_fs = load(fstore.at[c], HF.at[z, x, c])
    l_ft = load(features, GF.at[pl.ds(grp * 8, 8)])
    l_hs = load(hstore.at[c], HH.at[z, x, c])
    l_ta = load(gtiles, TA)
    l_tb = load(htiles, TB)
    l_ct = load(cot_h, COT)
    l_w = [
        load(s1_h, W1.at[pl.ds(0, 128)]), load(n1_h, W1.at[pl.ds(128, 128)]),
        load(s2_h, W2.at[pl.ds(0, 256)]), load(n2_h, W2.at[pl.ds(256, 256)]),
    ]

    l_tbl = pltpu.make_async_copy(TBV, TBS, tb_sem)

    def slot_order():
        lane = lax.broadcasted_iota(I32, (8, 128), 1)
        sources = [gsrc[i // 8, i % 8] for i in range(64)]
        named_row = jnp.zeros((8, 128), I32)
        for i, s in enumerate(sources):
            named_row = jnp.where(lane == i, s, named_row)
        place = jnp.zeros((8, 128), I32)
        upto = jnp.zeros((8, 128), I32)
        many = jnp.zeros((8, 128), I32)
        for i, s in enumerate(sources):
            place = place + jnp.where((s < named_row) | ((s == named_row) & (lane > i)), 1, 0)
            upto = upto + jnp.where(lane >= s, 1, 0)
            many = many + jnp.where(lane == s, 1, 0)
        place_col = jnp.transpose(jnp.broadcast_to(place[0:1], (128, 128)))[:64]
        named_col = jnp.transpose(jnp.broadcast_to(named_row[0:1], (128, 128)))[:64]
        hit = place_col == lax.broadcasted_iota(I32, (64, 128), 1)
        order = jnp.sum(jnp.where(hit, lax.broadcasted_iota(I32, (64, 128), 0), 0), axis=0, keepdims=True)
        target = jnp.sum(jnp.where(hit, named_col, 0), axis=0, keepdims=True)
        target = jnp.broadcast_to(target, (8, 128))
        same = jnp.where((target == pltpu.roll(target, 1, 1)) & (lane > 0), 1, 0)
        TBV[0:1, :] = order
        TBV[1:2, :] = order >> 3
        TBV[2:3, :] = same[0:1]
        TBV[3:4, :] = jnp.maximum(upto - 1, 0)[0:1]
        TBV[4:5, :] = jnp.minimum(many, 1)[0:1]
        l_tbl.start()

    class Plane:
        def __init__(self, X, n, unit, flag):
            self.X, self.n, self.unit, self.flag = X, n, unit, flag
            cut = CUTS[n]
            self.rows = {"a": (0, cut), "b": (cut, 8 - cut)}
            self.left = 16

        def at(self, zi, xi, kind, part=None):
            first, rows = self.rows[kind]
            if part is not None:
                rows = rows // 2
                first = first + part * rows
            return self.X.at[zi, xi, c, pl.ds(first, rows)]

        def kib(self, kind, part):
            return self.rows[kind][1] * self.unit / (1 if part is None else 2)

        def go(self, link, zi, xi, arrive, kind, part, rs, then):
            r = self.at(zi, xi, kind, part)
            rank = 2 * self.n + int((kind == "a") == (link[0] == "z"))
            push(link, self.kib(kind, part), r, r, self.at(*arrive, kind, part), pl_s.at[self.n], rs, then, rank)

        def share(self, zi, kind):
            first, rows = self.rows[kind]
            r = self.X.at[zi, pl.ds(0, NX), c, pl.ds(first, rows)]
            self.left -= 1
            act = self.finish if self.left == 0 else lambda: None
            copy = remote(r, r, sib_s.at[self.n], sib_r.at[self.n], sib)
            plan.transfer("sib", 4 * self.kib(kind, None), copy.start, act)

        def finish(self):
            r = self.X.at[:, :, o]
            remote(r, r, sib_s.at[self.n], sib_r.at[self.n], sib).wait()
            plan.mark(self.flag)

        def x_ring(self, kind, d, sem, have, whole):
            n, state = self.n, {"halves": 0, "units": 1}

            def unit(dx):
                have(dx)
                state["units"] += 1
                if state["units"] == 4:
                    whole()

            def half():
                state["halves"] += 1
                if state["halves"] == 2:
                    unit(2)

            def first(s):
                def then():
                    link, part = ("x+", 0) if s == 1 else ("x-", 1)
                    self.go(link, zz(d), xx(-s), (zz(d), xx(2)), kind, part, sem(2 + part), half)
                    unit(-s)

                return then

            self.go("x+", zz(d), x, (zz(d), xx(-1)), kind, None, sem(0), first(1))
            self.go("x-", zz(d), x, (zz(d), xx(1)), kind, None, sem(1), first(-1))

        def z_ring(self, kind, dx, sem, have, whole):
            state = {"halves": 0}

            def half():
                state["halves"] += 1
                if state["halves"] == 2:
                    have(4)

            def hop(s, j):
                link = "z+" if s == 1 else "z-"
                part = None if j < 4 else (0 if s == 1 else 1)

                def then():
                    if j == 4:
                        half()
                        return
                    hop(s, j + 1)
                    have(-s * j)

                index = 2 * (j - 1) + (0 if s == 1 else 1)
                self.go(link, zz(-s * (j - 1)), xx(dx), (zz(-s * j), xx(dx)), kind, part, sem(index), then)

            hop(1, 1)
            hop(-1, 1)

        def start(self):
            n = self.n
            rows_a = {}

            def have_a(dz):
                rows_a[dz % NZ] = rows_a.get(dz % NZ, 0) + 1
                if rows_a[dz % NZ] == 4:
                    self.share(zz(dz), "a")

            def a_unit(dx):
                have_a(0)
                base = 8 * (dx % NX)
                self.z_ring("a", dx, lambda i: az_r.at[n, base + i], have_a, None)

            def b_unit(dz):
                base = 4 * (dz % NZ)
                self.x_ring(
                    "b", dz, lambda i: bx_r.at[n, base + i], lambda dx: None, lambda: self.share(zz(dz), "b")
                )

            self.z_ring("b", 0, lambda i: bz_r.at[n, i], b_unit, None)
            self.x_ring("a", 0, lambda i: ax_r.at[n, i], a_unit, lambda: None)
            b_unit(0)
            a_unit(0)

    class Ring:
        def __init__(self, X, n, out, kib, flag):
            self.X, self.n, self.out, self.kib, self.flag, self.left = X, n, out, kib, flag, 8

        def first(self, d, part):
            return (yy(d) * 2 + c) * 8 + 4 * part

        def at(self, d, part):
            return self.X.at[pl.ds(self.first(d, part), 4)]

        def go(self, s, d, part, index, then):
            link = "y+" if s == 1 else "y-"
            r = self.at(d, part)
            push(link, 128, r, r, self.at(d - s, part), y_s.at[self.n], y_r.at[self.n, index], then, 2 * self.n)

        def share(self, d, part):
            r = self.out.at[pl.ds(self.first(d, part), 4)]
            self.left -= 1
            act = self.finish if self.left == 0 else lambda: None
            copy = remote(r, r, sib_s.at[2 + self.n], sib_r.at[2 + self.n], sib)
            plan.transfer("sib", self.kib, copy.start, act)

        def have(self, d, part):
            if self.out is self.X:
                self.share(d, part)
                return

            def act():
                @pl.loop(0, 2)
                def _(j):
                    two = pl.ds(self.first(d, part) + 2 * j, 2)
                    both = jnp.concatenate([GF[two].reshape(256, 128), GM[two].reshape(256, 128)], axis=1)
                    pre = dot(both, W1[...])
                    GH[two] = (pre * sigmoid(pre)).astype(BF16).reshape(2, 128, 256)

                self.share(d, part)

            plan.job([], 400, act)

        def finish(self):
            r = self.out.at[pl.ds(0, 32)]
            remote(r, r, sib_s.at[2 + self.n], sib_r.at[2 + self.n], sib).wait()
            plan.mark(self.flag)

        def start(self, part):
            s = 1 - 2 * part

            def lead():
                self.go(s, -s, part, 4 + part, lambda: self.have(2, part))
                self.have(-s, part)

            self.go(s, 0, part, part, lead)
            self.go(-s, 0, part, 2 + part, lambda: self.have(s, part))
            self.share(0, part)

    def degrees(first, many):
        def act():
            @pl.loop(first, first + many)
            def _(k):
                near_live, far_live = gcnt[k], hcnt[k]
                total = jnp.zeros((128, 128), F32)
                for s in range(8):
                    t = TA[k * 8 + s].astype(F32) * jnp.where(s < near_live, 1.0, 0.0)
                    TA[k * 8 + s] = t.astype(BF16)
                    total = total + t
                for s in range(4):
                    t = TB[k * 4 + s].astype(F32) * jnp.where(s < far_live, 1.0, 0.0)
                    TB[k * 4 + s] = t.astype(BF16)
                    total = total + t
                inv = 1.0 / (1.0 + jnp.sum(total, axis=1, keepdims=True))
                INV[k] = jnp.broadcast_to(inv, (128, 128))
                SCT[k] = jnp.transpose(COT[k].astype(F32) * inv).astype(BF16)

        return act

    held = {}

    def terms(first, many):
        def term(i, acc):
            acc = acc * TBS[2, i].astype(F32) + dot(SCT[TBS[1, i]], TA[TBS[0, i]])
            RT[i] = acc.astype(BF16)
            return acc

        def act():
            start = held.get("acc")
            start = jnp.zeros((256, 128), F32) if start is None else start
            held["acc"] = lax.fori_loop(first, first + many, term, start, unroll=4)

        return act

    def partial(g):
        return RT[TBS[3, g]].astype(F32) * TBS[4, g].astype(F32)

    def for_sibling(d):
        def act():
            @pl.loop(0, 8)
            def _(i):
                PS[yy(d) * 8 + i] = partial((yy(d) * 2 + o) * 8 + i).astype(BF16)

            r = pl.ds(yy(d) * 8, 8)
            copy = remote(PS.at[r], PR.at[r], ps_s, ps_r.at[d], sib)

            def then():
                copy.wait_recv()
                plan.mark(f"PR{d}")

            plan.transfer("sib", 512, copy.start, then, -1)

        return act

    def piece(d, part):
        return Q.at[pl.ds(yy(d) * 8 + 4 * part, 4)]

    def back(link, src, dst, index, then):
        push(link, 256, src, dst, dst, rs_s, rs_r.at[index], then, 1)

    def combine(d):
        def act():
            @pl.loop(0, 8)
            def _(i):
                g = (yy(d) * 2 + c) * 8 + i
                Q[yy(d) * 8 + i] = (partial(g) + PR[yy(d) * 8 + i].astype(F32)).astype(BF16)

            if d == 2:
                back("y+", piece(2, 0), T1.at[0], 0, lambda: plan.mark("T0"))
                back("y-", piece(2, 1), T1.at[1], 1, lambda: plan.mark("T1"))
            elif d == 1:
                back("y+", piece(1, 1), FR.at[0, pl.ds(4, 4)], 2, lambda: plan.mark("R2"))
            elif d == 3:
                back("y-", piece(-1, 0), FR.at[1, pl.ds(0, 4)], 3, lambda: plan.mark("R3"))

        return act

    def onward(part):
        def act():
            d = 1 if part == 0 else -1

            @pl.loop(0, 4)
            def _(i):
                j = yy(d) * 8 + 4 * part + i
                Q[j] = (Q[j].astype(F32) + T1[part, i].astype(F32)).astype(BF16)

            link = "y+" if part == 0 else "y-"
            flag = "R4" if part == 0 else "R5"
            back(link, piece(d, part), FR.at[part, pl.ds(4 * part, 4)], 4 + part, lambda: plan.mark(flag))

        return act

    def side_by_side(X, k, many):
        return jnp.concatenate([X[k * many + s] for s in range(many)], axis=1)

    def stacked(blocks):
        return jnp.concatenate(blocks, axis=0)

    def near_one(first, many):
        def act():
            @pl.loop(first, first + many)
            def _(k):
                ACC[k] = dot(side_by_side(TA, k, 8), stacked([GF[gsrc[k, s]] for s in range(8)]))

        return act

    def far_of(X, k):
        blocks = []
        for s in range(4):
            w, l = howner[s, 0, k], hlocal[s, k]
            blocks += [X[w // 4, w % 4, l // 2, (l % 2) * 4 + i] for i in range(4)]
        return stacked(blocks)

    mean_ring = Ring(GM, 1, GH, 256, "GH")

    def far_one(first, many):
        def act():
            if first == 0:
                for w in l_w:
                    w.wait()

            @pl.loop(first, first + many)
            def _(k):
                total = ACC[k] + dot(side_by_side(TB, k, 4), far_of(HF, k))
                mean = (total * INV[k]).astype(BF16)
                GM[grp * 8 + k] = mean
                pre = dot(jnp.concatenate([GF[grp * 8 + k], mean], axis=1), W1[...])
                PRE[k] = pre
                GH[grp * 8 + k] = (pre * sigmoid(pre)).astype(BF16)

            if (first + many) % 4 == 0:
                mean_ring.start(first // 4)

        return act

    def turned():
        W2T[pl.ds(0, 256), :] = jnp.transpose(W2[pl.ds(0, 256), :].astype(F32)).astype(BF16)
        W2T[pl.ds(256, 256), :] = jnp.transpose(W2[pl.ds(256, 256), :].astype(F32)).astype(BF16)

    def scaled(total, inv):
        return jnp.concatenate([total[:, :128] * inv, total[:, 128:] * inv], axis=1).astype(BF16)

    def far_two(first, many):
        def act():
            @pl.loop(first, first + many)
            def _(k):
                total = dot(side_by_side(TB, k, 4), far_of(HH, k))
                FAR[k] = total
                MF[k] = scaled(total, INV[k])

        return act

    def returned(first, many):
        def act():
            @pl.loop(first, first + many)
            def _(k):
                r = Q[y * 8 + k].astype(F32) + FR[0, k].astype(F32) + FR[1, k].astype(F32)
                r = jnp.transpose(r).astype(BF16)
                RB[k] = r
                total = dot(jnp.concatenate([COT[k], r], axis=1), W2T[...])
                pre = PRE[k]
                sigma = sigmoid(pre)
                GP[k] = (total * sigma * (1.0 + pre * (1.0 - sigma))).astype(BF16)

        return act

    def own_hidden():
        return GH[pl.ds(grp * 8, 8)].reshape(1024, 256)

    def flat(X):
        return X[...].reshape(1024, 256)

    def put(first, rows, v):
        G[pl.ds(first, rows), :] = v[:, :128].astype(BF16)
        G[pl.ds(first + rows, rows), :] = v[:, 128:].astype(BF16)

    def gradients_one():
        own = pl.ds(grp * 8, 8)
        both = jnp.concatenate([GF[own].reshape(1024, 128), GM[own].reshape(1024, 128)], axis=1)
        v = dot_t(both, flat(GP))
        put(0, 128, v[:128])
        put(256, 128, v[128:])

    def gradient_self_two():
        put(512, 256, dot_t(own_hidden(), flat(COT)))

    def gradient_neigh_two():
        put(1536, 256, dot_t(flat(MF), flat(COT)))

    def gradient_neigh_near():
        put(1024, 256, dot_t(own_hidden(), flat(RB)))

    def wait_all(copies, flag):
        def then():
            for cp in copies:
                cp.wait_recv()
            plan.mark(flag)

        return then

    waiting = []

    def exchange(copies, cost, flag, link="all"):
        for src, dst, ss, rs, dev, arrives in copies:
            cp = remote(src, dst, ss, rs, dev)
            cp.start()
            waiting.append(cp)
        plan.now += 40 * len(copies)
        plan.later(plan.now + cost, wait_all([remote(a, a, ss, rs, dev) for _, _, ss, rs, dev, a in copies], flag))

    around = [(dy, dx) for dy in range(NY) for dx in range(NX) if (dy, dx) != (0, 0)]

    class Total:
        def __init__(self, n, first, rows):
            self.n, self.first, self.half, self.piece = n, first, rows // 2, rows // 32
            self.some = pl.ds(n * 48, self.piece)

        def rows(self, dy, dx):
            return pl.ds(self.first + c * self.half + yy(dy) * 4 * self.piece + xx(dx) * self.piece, self.piece)

        def core(self, core):
            return pl.ds(self.first + core * self.half, self.half)

        def reduce_sib(self):
            n, r = self.n, pl.ds(self.first // 2, self.half)
            exchange([(G.at[self.core(o)], B1.at[r], a_s.at[n, 0], a_r.at[n, 0], sib, B1.at[r])], 1100, f"B1{n}")

        def reduce_xy(self):
            n, r = self.n, self.core(c)
            Q1[r, :] = (G[r, :].astype(F32) + B1[pl.ds(self.first // 2, self.half), :].astype(F32)).astype(BF16)
            exchange(
                [
                    (
                        Q1.at[self.rows(dy, dx)], B2.at[i, self.some], b2s.at[n, i], b2r.at[n, i],
                        at(dy=dy, dx=dx), B2.at[i, self.some],
                    )
                    for i, (dy, dx) in enumerate(around)
                ],
                4500, f"B2{n}",
            )

        def reduce_z(self):
            n = self.n
            total = Q1[self.rows(0, 0), :].astype(F32)
            for i in range(15):
                total = total + B2[i, self.some, :].astype(F32)
            B4[z, self.some, :] = total.astype(BF16)
            exchange(
                [
                    (
                        B4.at[z, self.some], B4.at[z, self.some], b4s.at[n, d - 1], b4r.at[n, d - 1],
                        at(dz=d), B4.at[zz(-d), self.some],
                    )
                    for d in range(1, NZ)
                ],
                4800, f"B4{n}",
            )

        def gather_xy(self):
            n = self.n
            total = B4[0, self.some, :].astype(F32)
            for i in range(1, NZ):
                total = total + B4[i, self.some, :].astype(F32)
            r = self.rows(0, 0)
            FG[r, :] = total.astype(BF16)
            exchange(
                [
                    (FG.at[r], FG.at[r], b5s.at[n, i], b5r.at[n, i], at(dy=dy, dx=dx), FG.at[self.rows(-dy, -dx)])
                    for i, (dy, dx) in enumerate(around)
                ],
                4500, f"B5{n}",
            )

        def gather_sib(self):
            n, mine, other = self.n, FG.at[self.core(c)], FG.at[self.core(o)]
            exchange([(mine, mine, a_s.at[n, 1], a_r.at[n, 1], sib, other)], 1100, f"FG{n}")

        def jobs(self, needs):
            n = self.n
            plan.job([f"B5{n}"], 50, self.gather_sib)
            plan.job([f"B4{n}"], 100, self.gather_xy)
            plan.job([f"B2{n}"], 100, self.reduce_z)
            plan.job([f"B1{n}"], 150, self.reduce_xy)
            plan.job(needs, 50, self.reduce_sib)

    def near_two(first, many):
        def act():
            @pl.loop(first, first + many)
            def _(k):
                total = FAR[k] + dot(side_by_side(TA, k, 8), stacked([GH[gsrc[k, s]] for s in range(8)]))
                m = scaled(total, INV[k])
                emb[k] = dot(jnp.concatenate([GH[grp * 8 + k], m], axis=1), W2[...]).astype(BF16)

        return act

    def start():
        slot_order()
        l_fs.wait()
        l_ft.wait()
        pl.semaphore_wait(barrier, len(partners))
        Plane(HF, 0, 8, "HF").start()
        first_ring = Ring(GF, 0, GF, 128, "GF")
        first_ring.start(0)
        first_ring.start(1)

        def second():
            l_hs.wait()
            Plane(HH, 1, 16, "HH").start()

        plan.later(plan.now + 300, second)

    def first_wait():
        l_ta.wait()
        l_tb.wait()
        l_ct.wait()

    start()
    Total(1, 1536, 512).jobs(["gn2"])
    Total(0, 0, 1536).jobs(["g1", "gs2", "gnn"])
    plan.job([], 50, first_wait, "in")
    plan.job(["in"], 800, degrees(0, 4), "d0")
    plan.job(["d0"], 800, degrees(4, 4), "deg")
    plan.job(["T0", "q1"], 200, onward(0))
    plan.job(["T1", "q3"], 200, onward(1))
    for i in range(4):
        plan.job(["HF", f"o{i - 1}" if i else "n1"], 750, far_one(2 * i, 2), f"o{i}" if i < 3 else "own")
    plan.job(["deg"], 50, l_tbl.wait, "tbl")
    for i in range(8):
        plan.job([f"t{i - 1}" if i else "tbl"], 500, terms(8 * i, 8), f"t{i}")
    for d in (2, 1, 3, 0):
        plan.job(["t7"], 150, for_sibling(d))
    for d in (2, 1, 3, 0):
        plan.job([f"PR{d}"], 300, combine(d), f"q{d}")
    plan.job(["GF", "deg"], 900, near_one(0, 4), "n0")
    plan.job(["n0"], 900, near_one(4, 4), "n1")
    plan.job(["own"], 300, turned, "W2T")
    plan.job(["HH"], 800, far_two(0, 4), "f0")
    plan.job(["f0"], 800, far_two(4, 4), "f1")
    plan.job(["f1"], 700, gradient_neigh_two, "gn2")
    for i in range(4):
        plan.job(["R2", "R3", "R4", "R5", "q0", f"r{i - 1}" if i else "W2T"], 550, returned(2 * i, 2), f"r{i}" if i < 3 else "RB")
    plan.job(["RB"], 900, gradients_one, "g1")
    plan.job(["RB"], 900, gradient_neigh_near, "gnn")
    plan.job(["own"], 900, gradient_self_two, "gs2")
    for i in range(4):
        plan.job([f"e{i - 1}" if i else "GH", "f1"], 1000, near_two(2 * i, 2), f"e{i}")
    plan.run()

    grads[...] = FG[...]
    for n in range(2):
        X = (GF, GH)[n].at[pl.ds(0, 62)]
        remote(X, X, pl_s.at[n], az_r.at[n, 0], sib).wait_send()
        X = GF.at[pl.ds(0, 24)]
        remote(X, X, y_s.at[n], y_r.at[n, 0], sib).wait_send()
    X = Q.at[pl.ds(0, 24)]
    remote(X, X, rs_s, rs_r.at[0], sib).wait_send()
    remote(PS, PR, ps_s, ps_r.at[0], sib).wait_send()
    for cp in waiting:
        cp.wait_send()


def last_kernel(emb_in, grads, emb, gs1, gn1, gs2, gn2):
    emb[...] = emb_in[...]

    def take(first, rows, out):
        out[:, :128] = grads[pl.ds(first, rows), :].astype(F32)
        out[:, 128:] = grads[pl.ds(first + rows, rows), :].astype(F32)

    take(0, 128, gs1)
    take(256, 128, gn1)
    take(512, 256, gs2)
    take(1024, 256, gn2)
    gn2[:, :128] += grads[pl.ds(1536, 256), :].astype(F32)
    gn2[:, 128:] += grads[pl.ds(1792, 256), :].astype(F32)


def body(
    features, group_src, group_count, group_tiles, hist_owner, hist_local, hist_count, hist_tiles,
    feature_store, hidden_store, self_one, neigh_one, self_two, neigh_two, cotangent,
):
    anywhere = pl.BlockSpec(memory_space=pl.ANY)
    vmem = pl.BlockSpec(memory_space=pltpu.VMEM)
    smem = pl.BlockSpec(memory_space=pltpu.SMEM)
    V, D = pltpu.VMEM, pltpu.SemaphoreType.DMA
    scratch = [
        V((64, 128, 128), BF16), V((64, 128, 128), BF16), V((64, 128, 256), BF16),
        V((8, 4, 2, 8, 32, 128), BF16), V((8, 4, 2, 8, 32, 256), BF16),
        V((64, 128, 128), BF16), V((32, 128, 128), BF16), V((8, 128, 256), BF16),
        V((256, 256), BF16), V((512, 256), BF16), V((512, 256), BF16),
        V((8, 128, 128), F32), V((8, 256, 128), BF16), V((64, 256, 128), BF16),
        V((32, 256, 128), BF16), V((32, 256, 128), BF16), V((32, 256, 128), BF16),
        V((2, 4, 256, 128), BF16), V((2, 8, 256, 128), BF16), V((8, 128, 256), BF16),
        V((8, 128, 128), F32), V((8, 128, 256), F32),
        V((8, 128, 256), F32), V((8, 128, 256), BF16), V((8, 128, 256), BF16),
        V((2048, 128), BF16), V((1024, 128), BF16), V((2048, 128), BF16),
        V((15, 64, 128), BF16), V((8, 64, 128), BF16),
        V((2048, 128), BF16), V((8, 128), I32), pltpu.SMEM((8, 128), I32),
        D((12,)), D, D((4,)), D((4,)), D((2,)),
        D((2, 32)), D((2, 4)), D((2, 8)), D((2, 32)), D((2,)), D((2, 6)), D, D((6,)), D, D((4,)),
        D((2, 2)), D((2, 2)), D((2, 15)), D((2, 15)), D((2, 7)), D((2, 7)), D((2, 15)), D((2, 15)),
    ]
    emb, grads = pl.pallas_call(
        main_kernel,
        out_shape=(jax.ShapeDtypeStruct((8, 128, 256), BF16), jax.ShapeDtypeStruct((2048, 128), BF16)),
        in_specs=[smem] * 5 + [anywhere] * 10,
        out_specs=(vmem, vmem),
        scratch_shapes=scratch,
        compiler_params=pltpu.CompilerParams(
            collective_id=0, has_side_effects=True, vmem_limit_bytes=60 * 2**20
        ),
    )(
        group_src, group_count, hist_owner.transpose(1, 2, 0), hist_local.T, hist_count,
        features, group_tiles.reshape(64, 128, 128), hist_tiles.reshape(32, 128, 128),
        feature_store.reshape(2, 8, 32, 128), hidden_store.reshape(2, 8, 32, 256),
        self_one, neigh_one, self_two, neigh_two, cotangent,
    )
    return pl.pallas_call(
        last_kernel,
        out_shape=(
            jax.ShapeDtypeStruct((8, 128, 256), BF16),
            jax.ShapeDtypeStruct((128, 256), F32),
            jax.ShapeDtypeStruct((128, 256), F32),
            jax.ShapeDtypeStruct((256, 256), F32),
            jax.ShapeDtypeStruct((256, 256), F32),
        ),
        in_specs=[vmem] * 2,
        out_specs=(vmem,) * 5,
    )(emb, grads)


def solution(mesh):
    every = P(("grp", "wide"))
    wide = P("wide")
    placed = (every,) * 8 + (wide, wide) + (P(),) * 4 + (every,)
    return jax.shard_map(
        body, mesh=mesh, in_specs=placed, out_specs=(every, P(), P(), P(), P()), check_vma=False
    )
```

```python
import heapq

import jax
import jax.numpy as jnp
from jax import lax
from jax.experimental import pallas as pl
from jax.experimental.pallas import tpu as pltpu
from jax.sharding import PartitionSpec as P

MESH = pl.DeviceIdType.MESH
F32 = jnp.float32
BF16 = jnp.bfloat16
I32 = jnp.int32
NX, NY, NZ = 4, 4, 8
CUTS = (2, 4)


def dot(a, b):
    return jnp.dot(a, b, preferred_element_type=F32)


def dot_t(a, b):
    return lax.dot_general(a, b, (((0,), (0,)), ((), ())), preferred_element_type=F32)


def sigmoid(v):
    return 0.5 + 0.5 * jnp.tanh(0.5 * v)


class Plan:
    RATE = {"sib": 2.0}
    LATENCY = {"sib": 1000}
    AHEAD = 2000

    def __init__(self):
        self.now, self.count = 0.0, 0
        self.heap, self.jobs, self.done, self.busy, self.queue = [], [], set(), {}, {}

    def later(self, time, act):
        heapq.heappush(self.heap, (time, self.count, act))
        self.count += 1

    def transfer(self, link, kib, start, act, rank=0):
        queue = self.queue.setdefault(link, [])
        heapq.heappush(queue, (rank, self.count, kib, start, act))
        self.count += 1
        if len(queue) == 1:
            self.pump(link)

    def pump(self, link):
        queue = self.queue[link]
        while queue:
            free = self.busy.get(link, 0.0) - self.AHEAD
            if free > self.now:
                self.later(free, lambda: self.pump(link))
                return
            _, _, kib, start, act = heapq.heappop(queue)
            start()
            self.now += 15
            end = max(self.now, self.busy.get(link, 0.0)) + kib * self.RATE.get(link, 22.0)
            self.busy[link] = end
            self.later(end + self.LATENCY.get(link, 1500), act)

    def job(self, needs, cost, act, gives=None):
        self.jobs.append((set(needs), cost, act, gives))

    def mark(self, flag):
        self.done.add(flag)

    def run(self):
        while self.heap or self.jobs:
            if self.heap and self.heap[0][0] <= self.now:
                self.now += 15
                heapq.heappop(self.heap)[2]()
                continue
            ready = [j for j in self.jobs if j[0] <= self.done]
            if ready:
                job = ready[0]
                self.jobs.remove(job)
                job[2]()
                self.now += job[1]
                if job[3] is not None:
                    self.done.add(job[3])
            else:
                self.now = self.heap[0][0]


def main_kernel(
    gsrc, gcnt, howner, hlocal, hcnt, features, gtiles, htiles, fstore, hstore, s1_h, n1_h, s2_h, n2_h, cot_h,
    emb, FG,
    GF, GM, GH, HF, HH, TA, TB, COT, W1, W2, W2T,
    INV, SCT, RT, PS, PR, Q, T1, FR, RB, ACC, PRE, FAR, MF, GP,
    G, GN, B1, Q1, B2, B4, EB, TBV, TBS,
    out_sem, load_sem, tb_sem, sib_s, sib_r, pl_s, az_r, ax_r, bz_r, bx_r, y_s, y_r, rs_s, rs_r, ps_s, ps_r,
    a_s, a_r, b2s, b2r, b4s, b4r, b5s, b5r,
):
    grp = lax.axis_index("grp")
    wide = lax.axis_index("wide")
    z, x = wide // NX, wide % NX
    y, c = grp // 2, grp % 2
    o = 1 - c
    plan = Plan()

    def zz(d):
        return (z + d) % NZ

    def xx(d):
        return (x + d) % NX

    def yy(d):
        return (y + d) % NY

    def at(dz=0, dy=0, dx=0):
        return (yy(dy) * 2 + c, zz(dz) * NX + xx(dx))

    sib = (y * 2 + o, wide)
    STEP = {"x+": at(dx=1), "x-": at(dx=-1), "y+": at(dy=1), "y-": at(dy=-1), "z+": at(dz=1), "z-": at(dz=-1)}

    def remote(src, dst, ss, rs, dev):
        return pltpu.make_async_remote_copy(
            src_ref=src, dst_ref=dst, send_sem=ss, recv_sem=rs, device_id=dev, device_id_type=MESH
        )

    def push(link, kib, src, dst, arrives, ss, rs, then, rank):
        def arrived():
            remote(arrives, arrives, ss, rs, sib).wait_recv()
            then()

        plan.transfer(link, kib, remote(src, dst, ss, rs, STEP[link]).start, arrived, rank)

    partners = [sib]
    partners += [at(dy=dy, dx=dx) for dy in range(NY) for dx in range(NX) if (dy, dx) != (0, 0)]
    partners += [at(dz=d) for d in range(1, NZ)]
    barrier = pltpu.get_barrier_semaphore()
    for p in partners:
        pl.semaphore_signal(barrier, inc=1, device_id=p, device_id_type=MESH)

    loads = []

    def load(src, dst):
        cp = pltpu.make_async_copy(src, dst, load_sem.at[len(loads)])
        cp.start()
        loads.append(cp)
        return cp

    l_fs = load(fstore.at[c], HF.at[z, x, c])
    l_ft = load(features, GF.at[pl.ds(grp * 8, 8)])
    l_hs = load(hstore.at[c], HH.at[z, x, c])
    l_ta = load(gtiles, TA)
    l_tb = load(htiles, TB)
    l_ct = load(cot_h, COT)
    l_w = [
        load(s1_h, W1.at[pl.ds(0, 128)]), load(n1_h, W1.at[pl.ds(128, 128)]),
        load(s2_h, W2.at[pl.ds(0, 256)]), load(n2_h, W2.at[pl.ds(256, 256)]),
    ]

    l_tbl = pltpu.make_async_copy(TBV, TBS, tb_sem)

    def slot_order():
        lane = lax.broadcasted_iota(I32, (8, 128), 1)
        sources = [gsrc[i // 8, i % 8] for i in range(64)]
        named_row = jnp.zeros((8, 128), I32)
        for i, s in enumerate(sources):
            named_row = jnp.where(lane == i, s, named_row)
        place = jnp.zeros((8, 128), I32)
        upto = jnp.zeros((8, 128), I32)
        many = jnp.zeros((8, 128), I32)
        for i, s in enumerate(sources):
            place = place + jnp.where((s < named_row) | ((s == named_row) & (lane > i)), 1, 0)
            upto = upto + jnp.where(lane >= s, 1, 0)
            many = many + jnp.where(lane == s, 1, 0)
        place_col = jnp.transpose(jnp.broadcast_to(place[0:1], (128, 128)))[:64]
        named_col = jnp.transpose(jnp.broadcast_to(named_row[0:1], (128, 128)))[:64]
        hit = place_col == lax.broadcasted_iota(I32, (64, 128), 1)
        order = jnp.sum(jnp.where(hit, lax.broadcasted_iota(I32, (64, 128), 0), 0), axis=0, keepdims=True)
        target = jnp.sum(jnp.where(hit, named_col, 0), axis=0, keepdims=True)
        target = jnp.broadcast_to(target, (8, 128))
        same = jnp.where((target == pltpu.roll(target, 1, 1)) & (lane > 0), 1, 0)
        TBV[0:1, :] = order
        TBV[1:2, :] = order >> 3
        TBV[2:3, :] = same[0:1]
        TBV[3:4, :] = jnp.maximum(upto - 1, 0)[0:1]
        TBV[4:5, :] = jnp.minimum(many, 1)[0:1]
        l_tbl.start()

    class Plane:
        def __init__(self, X, n, unit, flag):
            self.X, self.n, self.unit, self.flag = X, n, unit, flag
            cut = CUTS[n]
            self.rows = {"a": (0, cut), "b": (cut, 8 - cut)}
            self.left = 16

        def at(self, zi, xi, kind, part=None):
            first, rows = self.rows[kind]
            if part is not None:
                rows = rows // 2
                first = first + part * rows
            return self.X.at[zi, xi, c, pl.ds(first, rows)]

        def kib(self, kind, part):
            return self.rows[kind][1] * self.unit / (1 if part is None else 2)

        def go(self, link, zi, xi, arrive, kind, part, rs, then):
            r = self.at(zi, xi, kind, part)
            rank = 2 * self.n + int((kind == "a") == (link[0] == "z"))
            push(link, self.kib(kind, part), r, r, self.at(*arrive, kind, part), pl_s.at[self.n], rs, then, rank)

        def share(self, zi, kind):
            first, rows = self.rows[kind]
            r = self.X.at[zi, pl.ds(0, NX), c, pl.ds(first, rows)]
            self.left -= 1
            act = self.finish if self.left == 0 else lambda: None
            copy = remote(r, r, sib_s.at[self.n], sib_r.at[self.n], sib)
            plan.transfer("sib", 4 * self.kib(kind, None), copy.start, act)

        def finish(self):
            r = self.X.at[:, :, o]
            remote(r, r, sib_s.at[self.n], sib_r.at[self.n], sib).wait()
            plan.mark(self.flag)

        def x_ring(self, kind, d, sem, have, whole):
            n, state = self.n, {"halves": 0, "units": 1}

            def unit(dx):
                have(dx)
                state["units"] += 1
                if state["units"] == 4:
                    whole()

            def half():
                state["halves"] += 1
                if state["halves"] == 2:
                    unit(2)

            def first(s):
                def then():
                    link, part = ("x+", 0) if s == 1 else ("x-", 1)
                    self.go(link, zz(d), xx(-s), (zz(d), xx(2)), kind, part, sem(2 + part), half)
                    unit(-s)

                return then

            self.go("x+", zz(d), x, (zz(d), xx(-1)), kind, None, sem(0), first(1))
            self.go("x-", zz(d), x, (zz(d), xx(1)), kind, None, sem(1), first(-1))

        def z_ring(self, kind, dx, sem, have, whole):
            state = {"halves": 0}

            def half():
                state["halves"] += 1
                if state["halves"] == 2:
                    have(4)

            def hop(s, j):
                link = "z+" if s == 1 else "z-"
                part = None if j < 4 else (0 if s == 1 else 1)

                def then():
                    if j == 4:
                        half()
                        return
                    hop(s, j + 1)
                    have(-s * j)

                index = 2 * (j - 1) + (0 if s == 1 else 1)
                self.go(link, zz(-s * (j - 1)), xx(dx), (zz(-s * j), xx(dx)), kind, part, sem(index), then)

            hop(1, 1)
            hop(-1, 1)

        def start(self):
            n = self.n
            rows_a = {}

            def have_a(dz):
                rows_a[dz % NZ] = rows_a.get(dz % NZ, 0) + 1
                if rows_a[dz % NZ] == 4:
                    self.share(zz(dz), "a")

            def a_unit(dx):
                have_a(0)
                base = 8 * (dx % NX)
                self.z_ring("a", dx, lambda i: az_r.at[n, base + i], have_a, None)

            def b_unit(dz):
                base = 4 * (dz % NZ)
                self.x_ring(
                    "b", dz, lambda i: bx_r.at[n, base + i], lambda dx: None, lambda: self.share(zz(dz), "b")
                )

            self.z_ring("b", 0, lambda i: bz_r.at[n, i], b_unit, None)
            self.x_ring("a", 0, lambda i: ax_r.at[n, i], a_unit, lambda: None)
            b_unit(0)
            a_unit(0)

    class Ring:
        def __init__(self, X, n, out, kib, flag):
            self.X, self.n, self.out, self.kib, self.flag, self.left = X, n, out, kib, flag, 8

        def first(self, d, part):
            return (yy(d) * 2 + c) * 8 + 4 * part

        def at(self, d, part):
            return self.X.at[pl.ds(self.first(d, part), 4)]

        def go(self, s, d, part, index, then):
            link = "y+" if s == 1 else "y-"
            r = self.at(d, part)
            push(link, 128, r, r, self.at(d - s, part), y_s.at[self.n], y_r.at[self.n, index], then, 2 * self.n)

        def share(self, d, part):
            r = self.out.at[pl.ds(self.first(d, part), 4)]
            self.left -= 1
            act = self.finish if self.left == 0 else lambda: None
            copy = remote(r, r, sib_s.at[2 + self.n], sib_r.at[2 + self.n], sib)
            plan.transfer("sib", self.kib, copy.start, act)

        def have(self, d, part):
            if self.out is self.X:
                self.share(d, part)
                return

            def act():
                @pl.loop(0, 2)
                def _(j):
                    two = pl.ds(self.first(d, part) + 2 * j, 2)
                    both = jnp.concatenate([GF[two].reshape(256, 128), GM[two].reshape(256, 128)], axis=1)
                    pre = dot(both, W1[...])
                    GH[two] = (pre * sigmoid(pre)).astype(BF16).reshape(2, 128, 256)

                self.share(d, part)

            plan.job([], 400, act)

        def finish(self):
            r = self.out.at[pl.ds(0, 32)]
            remote(r, r, sib_s.at[2 + self.n], sib_r.at[2 + self.n], sib).wait()
            plan.mark(self.flag)

        def start(self, part):
            s = 1 - 2 * part

            def lead():
                self.go(s, -s, part, 4 + part, lambda: self.have(2, part))
                self.have(-s, part)

            self.go(s, 0, part, part, lead)
            self.go(-s, 0, part, 2 + part, lambda: self.have(s, part))
            self.share(0, part)

    def degrees(first, many):
        def act():
            @pl.loop(first, first + many)
            def _(k):
                near_live, far_live = gcnt[k], hcnt[k]
                total = jnp.zeros((128, 128), F32)
                for s in range(8):
                    t = TA[k * 8 + s].astype(F32) * jnp.where(s < near_live, 1.0, 0.0)
                    TA[k * 8 + s] = t.astype(BF16)
                    total = total + t
                for s in range(4):
                    t = TB[k * 4 + s].astype(F32) * jnp.where(s < far_live, 1.0, 0.0)
                    TB[k * 4 + s] = t.astype(BF16)
                    total = total + t
                inv = 1.0 / (1.0 + jnp.sum(total, axis=1, keepdims=True))
                INV[k] = jnp.broadcast_to(inv, (128, 128))
                SCT[k] = jnp.transpose(COT[k].astype(F32) * inv).astype(BF16)

        return act

    held = {}

    def terms(first, many):
        def term(i, acc):
            acc = acc * TBS[2, i].astype(F32) + dot(SCT[TBS[1, i]], TA[TBS[0, i]])
            RT[i] = acc.astype(BF16)
            return acc

        def act():
            start = held.get("acc")
            start = jnp.zeros((256, 128), F32) if start is None else start
            held["acc"] = lax.fori_loop(first, first + many, term, start, unroll=4)

        return act

    def partial(g):
        return RT[TBS[3, g]].astype(F32) * TBS[4, g].astype(F32)

    def for_sibling(d):
        def act():
            @pl.loop(0, 8)
            def _(i):
                PS[yy(d) * 8 + i] = partial((yy(d) * 2 + o) * 8 + i).astype(BF16)

            r = pl.ds(yy(d) * 8, 8)
            copy = remote(PS.at[r], PR.at[r], ps_s, ps_r.at[d], sib)

            def then():
                copy.wait_recv()
                plan.mark(f"PR{d}")

            plan.transfer("sib", 512, copy.start, then, -1)

        return act

    def piece(d, part):
        return Q.at[pl.ds(yy(d) * 8 + 4 * part, 4)]

    def back(link, src, dst, index, then):
        push(link, 256, src, dst, dst, rs_s, rs_r.at[index], then, 1)

    def combine(d):
        def act():
            @pl.loop(0, 8)
            def _(i):
                g = (yy(d) * 2 + c) * 8 + i
                Q[yy(d) * 8 + i] = (partial(g) + PR[yy(d) * 8 + i].astype(F32)).astype(BF16)

            if d == 2:
                back("y+", piece(2, 0), T1.at[0], 0, lambda: plan.mark("T0"))
                back("y-", piece(2, 1), T1.at[1], 1, lambda: plan.mark("T1"))
            elif d == 1:
                back("y+", piece(1, 1), FR.at[0, pl.ds(4, 4)], 2, lambda: plan.mark("R2"))
            elif d == 3:
                back("y-", piece(-1, 0), FR.at[1, pl.ds(0, 4)], 3, lambda: plan.mark("R3"))

        return act

    def onward(part):
        def act():
            d = 1 if part == 0 else -1

            @pl.loop(0, 4)
            def _(i):
                j = yy(d) * 8 + 4 * part + i
                Q[j] = (Q[j].astype(F32) + T1[part, i].astype(F32)).astype(BF16)

            link = "y+" if part == 0 else "y-"
            flag = "R4" if part == 0 else "R5"
            back(link, piece(d, part), FR.at[part, pl.ds(4 * part, 4)], 4 + part, lambda: plan.mark(flag))

        return act

    def side_by_side(X, k, many):
        return jnp.concatenate([X[k * many + s] for s in range(many)], axis=1)

    def stacked(blocks):
        return jnp.concatenate(blocks, axis=0)

    def near_one(first, many):
        def act():
            @pl.loop(first, first + many)
            def _(k):
                ACC[k] = dot(side_by_side(TA, k, 8), stacked([GF[gsrc[k, s]] for s in range(8)]))

        return act

    def far_of(X, k):
        blocks = []
        for s in range(4):
            w, l = howner[s, 0, k], hlocal[s, k]
            blocks += [X[w // 4, w % 4, l // 2, (l % 2) * 4 + i] for i in range(4)]
        return stacked(blocks)

    mean_ring = Ring(GM, 1, GH, 256, "GH")

    def far_one(first, many):
        def act():
            if first == 0:
                for w in l_w:
                    w.wait()

            @pl.loop(first, first + many)
            def _(k):
                total = ACC[k] + dot(side_by_side(TB, k, 4), far_of(HF, k))
                mean = (total * INV[k]).astype(BF16)
                GM[grp * 8 + k] = mean
                pre = dot(jnp.concatenate([GF[grp * 8 + k], mean], axis=1), W1[...])
                PRE[k] = pre
                GH[grp * 8 + k] = (pre * sigmoid(pre)).astype(BF16)

            if (first + many) % 4 == 0:
                mean_ring.start(first // 4)

        return act

    def turned():
        W2T[pl.ds(0, 256), :] = jnp.transpose(W2[pl.ds(0, 256), :].astype(F32)).astype(BF16)
        W2T[pl.ds(256, 256), :] = jnp.transpose(W2[pl.ds(256, 256), :].astype(F32)).astype(BF16)

    def scaled(total, inv):
        return jnp.concatenate([total[:, :128] * inv, total[:, 128:] * inv], axis=1).astype(BF16)

    def far_two(first, many):
        def act():
            @pl.loop(first, first + many)
            def _(k):
                total = dot(side_by_side(TB, k, 4), far_of(HH, k))
                FAR[k] = total
                MF[k] = scaled(total, INV[k])

        return act

    def returned(first, many):
        def act():
            @pl.loop(first, first + many)
            def _(k):
                r = Q[y * 8 + k].astype(F32) + FR[0, k].astype(F32) + FR[1, k].astype(F32)
                r = jnp.transpose(r).astype(BF16)
                RB[k] = r
                total = dot(jnp.concatenate([COT[k], r], axis=1), W2T[...])
                pre = PRE[k]
                sigma = sigmoid(pre)
                GP[k] = (total * sigma * (1.0 + pre * (1.0 - sigma))).astype(BF16)

        return act

    def own_hidden():
        return GH[pl.ds(grp * 8, 8)].reshape(1024, 256)

    def flat(X):
        return X[...].reshape(1024, 256)

    def put(first, rows, v):
        G[pl.ds(first, rows), :] = v[:, :128].astype(BF16)
        G[pl.ds(first + rows, rows), :] = v[:, 128:].astype(BF16)

    def gradients_one():
        own = pl.ds(grp * 8, 8)
        both = jnp.concatenate([GF[own].reshape(1024, 128), GM[own].reshape(1024, 128)], axis=1)
        v = dot_t(both, flat(GP))
        put(0, 128, v[:128])
        put(256, 128, v[128:])

    def gradient_self_two():
        put(1024, 256, dot_t(own_hidden(), flat(COT)))

    def gradient_neigh_two():
        put(512, 256, GN[...] + dot_t(flat(MF), flat(COT)))

    def gradient_neigh_near():
        GN[...] = dot_t(own_hidden(), flat(RB))

    def exchange(copies, cost, flag):
        sent = [remote(src, dst, ss, rs, dev) for src, dst, ss, rs, dev, _ in copies]
        for cp in sent:
            cp.start()

        def left():
            for cp in sent:
                cp.wait_send()

        def then():
            for _, _, ss, rs, dev, a in copies:
                remote(a, a, ss, rs, dev).wait_recv()
            plan.mark(flag)
            plan.job([], 50, left)

        plan.now += 20 * len(copies)
        plan.later(plan.now + cost, then)

    around = [(dy, dx) for dy in range(NY) for dx in range(NX) if (dy, dx) != (0, 0)]
    around.sort(key=lambda d: -min(d[0], NY - d[0]) - min(d[1], NX - d[1]))

    class Total:
        def __init__(self, n, first, rows):
            self.n, self.first, self.half, self.piece = n, first, rows // 2, rows // 32
            self.some = pl.ds(n * 16, self.piece)

        def rows(self, dy, dx):
            return pl.ds(self.first + c * self.half + yy(dy) * 4 * self.piece + xx(dx) * self.piece, self.piece)

        def core(self, core):
            return pl.ds(self.first + core * self.half, self.half)

        def reduce_sib(self):
            n, r = self.n, pl.ds(self.first // 2, self.half)
            exchange([(G.at[self.core(o)], B1.at[r], a_s.at[n, 0], a_r.at[n, 0], sib, B1.at[r])], 1100, f"B1{n}")

        def reduce_xy(self):
            n, r = self.n, self.core(c)
            Q1[r, :] = (G[r, :].astype(F32) + B1[pl.ds(self.first // 2, self.half), :].astype(F32)).astype(BF16)
            exchange(
                [
                    (
                        Q1.at[self.rows(dy, dx)], B2.at[i, self.some], b2s.at[n, i], b2r.at[n, i],
                        at(dy=dy, dx=dx), B2.at[i, self.some],
                    )
                    for i, (dy, dx) in enumerate(around)
                ],
                4500, f"B2{n}",
            )

        def reduce_z(self):
            n = self.n
            total = Q1[self.rows(0, 0), :].astype(F32)
            for i in range(15):
                total = total + B2[i, self.some, :].astype(F32)
            B4[z, self.some, :] = total.astype(BF16)
            exchange(
                [
                    (
                        B4.at[z, self.some], B4.at[z, self.some], b4s.at[n, d - 1], b4r.at[n, d - 1],
                        at(dz=d), B4.at[zz(-d), self.some],
                    )
                    for d in (4, 3, 5, 2, 6, 1, 7)
                ],
                4800, f"B4{n}",
            )

        def gather_xy(self):
            n = self.n
            total = B4[0, self.some, :].astype(F32)
            for i in range(1, NZ):
                total = total + B4[i, self.some, :].astype(F32)
            r = self.rows(0, 0)
            FG[r, :] = total.astype(BF16)
            exchange(
                [
                    (FG.at[r], FG.at[r], b5s.at[n, i], b5r.at[n, i], at(dy=dy, dx=dx), FG.at[self.rows(-dy, -dx)])
                    for i, (dy, dx) in enumerate(around)
                ],
                4500, f"B5{n}",
            )

        def gather_sib(self):
            n, mine, other = self.n, FG.at[self.core(c)], FG.at[self.core(o)]
            exchange([(mine, mine, a_s.at[n, 1], a_r.at[n, 1], sib, other)], 1100, f"FG{n}")

        def jobs(self, needs):
            n = self.n
            plan.job([f"B5{n}"], 50, self.gather_sib)
            plan.job([f"B4{n}"], 100, self.gather_xy)
            plan.job([f"B2{n}"], 100, self.reduce_z)
            plan.job([f"B1{n}"], 150, self.reduce_xy)
            plan.job(needs, 50, self.reduce_sib)

    writes = []

    def near_two(first, many):
        def act():
            @pl.loop(first, first + many)
            def _(k):
                total = FAR[k] + dot(side_by_side(TA, k, 8), stacked([GH[gsrc[k, s]] for s in range(8)]))
                m = scaled(total, INV[k])
                EB[k] = dot(jnp.concatenate([GH[grp * 8 + k], m], axis=1), W2[...]).astype(BF16)

            cp = pltpu.make_async_copy(EB.at[pl.ds(first, many)], emb.at[pl.ds(first, many)], out_sem.at[first])
            cp.start()
            writes.append(cp)

        return act

    def start():
        slot_order()
        l_fs.wait()
        l_ft.wait()
        pl.semaphore_wait(barrier, len(partners))
        Plane(HF, 0, 8, "HF").start()
        first_ring = Ring(GF, 0, GF, 128, "GF")
        first_ring.start(0)
        first_ring.start(1)

        def second():
            l_hs.wait()
            Plane(HH, 1, 16, "HH").start()

        plan.later(plan.now + 300, second)

    def first_wait():
        l_ta.wait()
        l_tb.wait()
        l_ct.wait()

    start()
    Total(1, 0, 1024).jobs(["g1", "gn2"])
    Total(0, 1024, 512).jobs(["gs2"])
    plan.job([], 50, first_wait, "in")
    plan.job(["in"], 800, degrees(0, 4), "d0")
    plan.job(["d0"], 800, degrees(4, 4), "deg")
    plan.job(["T0", "q1"], 200, onward(0))
    plan.job(["T1", "q3"], 200, onward(1))
    for i in range(4):
        plan.job(["HF", f"o{i - 1}" if i else "n1"], 750, far_one(2 * i, 2), f"o{i}" if i < 3 else "own")
    plan.job(["deg"], 50, l_tbl.wait, "tbl")
    for i in range(8):
        plan.job([f"t{i - 1}" if i else "tbl"], 500, terms(8 * i, 8), f"t{i}")
    for d in (2, 1, 3, 0):
        plan.job(["t7"], 150, for_sibling(d))
    for d in (2, 1, 3, 0):
        plan.job([f"PR{d}"], 300, combine(d), f"q{d}")
    plan.job(["GF", "deg"], 900, near_one(0, 4), "n0")
    plan.job(["n0"], 900, near_one(4, 4), "n1")
    plan.job(["own"], 900, gradient_self_two, "gs2")
    plan.job(["own"], 300, turned, "W2T")
    plan.job(["HH"], 800, far_two(0, 4), "f0")
    plan.job(["f0"], 800, far_two(4, 4), "f1")
    for i in range(4):
        plan.job(["R2", "R3", "R4", "R5", "q0", f"r{i - 1}" if i else "W2T"], 550, returned(2 * i, 2), f"r{i}" if i < 3 else "RB")
    plan.job(["RB"], 900, gradients_one, "g1")
    plan.job(["RB"], 900, gradient_neigh_near, "gnn")
    plan.job(["gnn", "f1"], 900, gradient_neigh_two, "gn2")
    for i in range(8):
        plan.job([f"e{i - 1}" if i else "GH", "f1"], 500, near_two(i, 1), f"e{i}")
    plan.run()

    for cp in writes:
        cp.wait()
    for n in range(2):
        X = (GF, GH)[n].at[pl.ds(0, 62)]
        remote(X, X, pl_s.at[n], az_r.at[n, 0], sib).wait_send()
        X = GF.at[pl.ds(0, 24)]
        remote(X, X, y_s.at[n], y_r.at[n, 0], sib).wait_send()
    X = Q.at[pl.ds(0, 24)]
    remote(X, X, rs_s, rs_r.at[0], sib).wait_send()
    remote(PS, PR, ps_s, ps_r.at[0], sib).wait_send()


def last_kernel(emb_in, grads, emb, gs1, gn1, gs2, gn2):
    emb[...] = emb_in[...]

    def take(first, rows, out):
        out[:, :128] = grads[pl.ds(first, rows), :].astype(F32)
        out[:, 128:] = grads[pl.ds(first + rows, rows), :].astype(F32)

    take(0, 128, gs1)
    take(256, 128, gn1)
    take(512, 256, gn2)
    take(1024, 256, gs2)


def body(
    features, group_src, group_count, group_tiles, hist_owner, hist_local, hist_count, hist_tiles,
    feature_store, hidden_store, self_one, neigh_one, self_two, neigh_two, cotangent,
):
    anywhere = pl.BlockSpec(memory_space=pl.ANY)
    vmem = pl.BlockSpec(memory_space=pltpu.VMEM)
    smem = pl.BlockSpec(memory_space=pltpu.SMEM)
    V, D = pltpu.VMEM, pltpu.SemaphoreType.DMA
    scratch = [
        V((64, 128, 128), BF16), V((64, 128, 128), BF16), V((64, 128, 256), BF16),
        V((8, 4, 2, 8, 32, 128), BF16), V((8, 4, 2, 8, 32, 256), BF16),
        V((64, 128, 128), BF16), V((32, 128, 128), BF16), V((8, 128, 256), BF16),
        V((256, 256), BF16), V((512, 256), BF16), V((512, 256), BF16),
        V((8, 128, 128), F32), V((8, 256, 128), BF16), V((64, 256, 128), BF16),
        V((32, 256, 128), BF16), V((32, 256, 128), BF16), V((32, 256, 128), BF16),
        V((2, 4, 256, 128), BF16), V((2, 8, 256, 128), BF16), V((8, 128, 256), BF16),
        V((8, 128, 128), F32), V((8, 128, 256), F32),
        V((8, 128, 256), F32), V((8, 128, 256), BF16), V((8, 128, 256), BF16),
        V((1536, 128), BF16), V((256, 256), F32), V((768, 128), BF16), V((1536, 128), BF16),
        V((15, 48, 128), BF16), V((8, 48, 128), BF16),
        V((8, 128, 256), BF16), V((8, 128), I32), pltpu.SMEM((8, 128), I32),
        D((8,)), D((12,)), D, D((4,)), D((4,)), D((2,)),
        D((2, 32)), D((2, 4)), D((2, 8)), D((2, 32)), D((2,)), D((2, 6)), D, D((6,)), D, D((4,)),
        D((2, 2)), D((2, 2)), D((2, 15)), D((2, 15)), D((2, 7)), D((2, 7)), D((2, 15)), D((2, 15)),
    ]
    emb, grads = pl.pallas_call(
        main_kernel,
        out_shape=(jax.ShapeDtypeStruct((8, 128, 256), BF16), jax.ShapeDtypeStruct((1536, 128), BF16)),
        in_specs=[smem] * 5 + [anywhere] * 10,
        out_specs=(anywhere, vmem),
        scratch_shapes=scratch,
        compiler_params=pltpu.CompilerParams(
            collective_id=0, has_side_effects=True, vmem_limit_bytes=60 * 2**20
        ),
    )(
        group_src, group_count, hist_owner.transpose(1, 2, 0), hist_local.T, hist_count,
        features, group_tiles.reshape(64, 128, 128), hist_tiles.reshape(32, 128, 128),
        feature_store.reshape(2, 8, 32, 128), hidden_store.reshape(2, 8, 32, 256),
        self_one, neigh_one, self_two, neigh_two, cotangent,
    )
    return pl.pallas_call(
        last_kernel,
        out_shape=(
            jax.ShapeDtypeStruct((8, 128, 256), BF16),
            jax.ShapeDtypeStruct((128, 256), F32),
            jax.ShapeDtypeStruct((128, 256), F32),
            jax.ShapeDtypeStruct((256, 256), F32),
            jax.ShapeDtypeStruct((256, 256), F32),
        ),
        in_specs=[vmem] * 2,
        out_specs=(vmem,) * 5,
    )(emb, grads)


def solution(mesh):
    every = P(("grp", "wide"))
    wide = P("wide")
    placed = (every,) * 8 + (wide, wide) + (P(),) * 4 + (every,)
    return jax.shard_map(
        body, mesh=mesh, in_specs=placed, out_specs=(every, P(), P(), P(), P()), check_vma=False
    )
```
